256 devices in a mesh: blk: 128 (over x, z, y_lo, core), rep: 2 (over y_hi).
Axes of the slice: x: 4, y: 4 (y_hi: 2, y_lo: 2; y = y_hi * 2 + y_lo), z: 8, core: 2. Of those that a mesh axis runs over, the one named last changes fastest.
Arguments:
- image_emb: bfloat16 [131072, 1152], P(('blk', 'rep')), may hold values from -0.19921875 to 0.19921875
- text_emb: bfloat16 [131072, 1152], P(('blk', 'rep')), may hold values from -0.19921875 to 0.19921875
- log_temp: float32 [], replicated, may hold values from 1 to 2
- bias: float32 [], replicated, may hold values from -2 to 0
Outputs:
- row_loss: float32 [131072], P(('blk', 'rep'))
- grad_image: float32 [131072, 1152], P(('blk', 'rep'))
- grad_text: float32 [131072, 1152], P(('blk', 'rep'))
The draws below stay inside these ranges and needn't reach their ends.
All inputs are finite; a program needn't handle non-finite values.
Results may differ from the reference program's by a relative error of at most 0.0042.
Values may be sent and summed in bfloat16 or wider, within the bound.
No kernel may reach another device: no remote copies, remote signals or barrier semaphores. Data moves between devices by JAX's collectives and lax.ppermute only.
A program may use at most 64 MiB of HBM per device.

```python
import jax
import jax.numpy as jnp
from jax import lax

D = 1152
ROWS = 512
STEPS = 4
TOKENS = 131072


def levels(key, shape, cuts, smallest, high):
    def one(dim, parts):
        draws = jax.random.uniform(jax.random.fold_in(jax.random.fold_in(key, 6), dim), (parts,), jnp.float32, smallest / len(cuts), high / len(cuts))
        return jnp.repeat(jnp.exp(draws), shape[dim] // parts).reshape((-1,) + (1,) * (len(shape) - dim - 1))

    loudness = one(*cuts[0])
    for cut in cuts[1:]:
        loudness = loudness * one(*cut)
    return loudness


def centred(own_key, shape, scale, reach, cuts=(), kind=jnp.bfloat16):
    values = scale * jax.random.normal(own_key, shape, jnp.float32)
    if cuts:
        values = values * levels(own_key, shape, cuts, -0.22, 0.18)
    return jnp.clip(values, -reach, reach).astype(kind)


def setup_inputs(seed: int = 0) -> dict:
    key_list = jax.random.split(jax.random.key(seed), 5)
    image_emb = centred(key_list[0], (TOKENS, D), 0.03, 0.19921875, ((0, 256),))
    text_emb = centred(key_list[1], (TOKENS, D), 0.03, 0.19921875, ((0, 256),))
    log_temp = jnp.clip(jax.random.uniform(key_list[2], (), jnp.float32, 1.0, 2.0), 1.0, 2.0)
    bias = jnp.clip(jax.random.uniform(key_list[3], (), jnp.float32, -2.0, 0.0), -2.0, 0.0)
    return dict(image_emb=image_emb, text_emb=text_emb, log_temp=log_temp, bias=bias)


EPSILON = 1e-06

def unit_rows(embedding):
    values = embedding.astype(jnp.float32)
    scale = lax.rsqrt(lax.optimization_barrier(jnp.sum(values * values, axis=-1, keepdims=True)) + EPSILON)
    return (values * scale, scale)

def to_low(values):
    rounded = lax.optimization_barrier(values.astype(jnp.bfloat16))
    return rounded.astype(jnp.float32)

def reference(image_emb, text_emb, log_temp, bias):
    block_count = TOKENS // ROWS
    image_unit, image_scale = unit_rows(image_emb)
    text_unit, text_scale = unit_rows(text_emb)
    image_blocks = to_low(image_unit).reshape(block_count, ROWS, D)
    text_blocks = to_low(text_unit).reshape(block_count, ROWS, D)
    temper = jnp.exp(log_temp)
    signs = 2.0 * jnp.eye(ROWS, dtype=jnp.float32) - 1.0
    losses = jnp.zeros((block_count, ROWS), jnp.float32)
    grad_img = jnp.zeros((block_count, ROWS, D), jnp.float32)
    grad_txt = jnp.zeros((block_count, ROWS, D), jnp.float32)
    for offset in range(STEPS):
        partner = jnp.roll(text_blocks, offset, axis=0)
        logits = temper * jnp.einsum('bid,bjd->bij', image_blocks, partner, precision=lax.Precision.HIGHEST) + bias
        labels = signs if offset == 0 else -jnp.ones_like(signs)
        losses = losses - lax.optimization_barrier(jnp.sum(jax.nn.log_sigmoid(labels * logits), axis=-1))
        weights = to_low(-labels * jax.nn.sigmoid(-labels * logits) * temper)
        grad_img = grad_img + jnp.einsum('bij,bjd->bid', weights, partner, precision=lax.Precision.HIGHEST)
        term = jnp.einsum('bij,bid->bjd', weights, image_blocks, precision=lax.Precision.HIGHEST)
        grad_txt = grad_txt + jnp.roll(term, -offset, axis=0)
    grad_img = grad_img.reshape(TOKENS, D)
    grad_txt = grad_txt.reshape(TOKENS, D)
    grad_image = image_scale * (grad_img - image_unit * lax.optimization_barrier(jnp.sum(image_unit * grad_img, axis=-1, keepdims=True)))
    grad_text = text_scale * (grad_txt - text_unit * lax.optimization_barrier(jnp.sum(text_unit * grad_txt, axis=-1, keepdims=True)))
    return (losses.reshape(TOKENS), grad_image, grad_text)
```

```python
import jax
import jax.numpy as jnp
from jax import lax
from jax.sharding import PartitionSpec as P

STEPS = 4

EPSILON = 1e-06


def shifted(x, axis, by):
    count = lax.axis_size(axis)
    return lax.ppermute(x, axis, [(i, (i + by) % count) for i in range(count)])


def unit_rows(embedding):
    values = embedding.astype(jnp.float32)
    scale = lax.rsqrt(jnp.sum(values * values, axis=-1, keepdims=True) + EPSILON)
    return (values * scale, scale)


def low_rows(embedding):
    return unit_rows(embedding)[0].astype(jnp.bfloat16)


def block_logits(image_low, text_low, temper, bias):
    product = lax.dot_general(
        image_low, text_low, (((1,), (1,)), ((), ())), preferred_element_type=jnp.float32
    )
    return temper * product + bias


def block_losses(logits, labels):
    return -jnp.sum(jax.nn.log_sigmoid(labels * logits), axis=-1)


def block_weights(logits, labels, temper):
    return (-labels * jax.nn.sigmoid(-labels * logits) * temper).astype(jnp.bfloat16)


def for_image(weights, text_low):
    return jnp.dot(weights, text_low, preferred_element_type=jnp.float32)


def for_text(weights, image_low):
    return lax.dot_general(
        weights, image_low, (((0,), (0,)), ((), ())), preferred_element_type=jnp.float32
    )


def unit_backward(unit, scale, grad_unit):
    return scale * (grad_unit - unit * jnp.sum(unit * grad_unit, axis=-1, keepdims=True))


def body(image_emb, text_emb, log_temp, bias):
    row_count = image_emb.shape[0]
    axes = ("blk", "rep")
    texts = [shifted(text_emb, axes, o) for o in range(1, STEPS)]
    images = [shifted(image_emb, axes, -o) for o in range(1, STEPS)]
    image_unit, image_scale = unit_rows(image_emb)
    text_unit, text_scale = unit_rows(text_emb)
    image_low = image_unit.astype(jnp.bfloat16)
    text_low = text_unit.astype(jnp.bfloat16)
    temper = jnp.exp(log_temp)
    positive = 2.0 * jnp.eye(row_count, dtype=jnp.float32) - 1.0
    negative = -jnp.ones((row_count, row_count), jnp.float32)
    logits = block_logits(image_low, text_low, temper, bias)
    losses = block_losses(logits, positive)
    weights = block_weights(logits, positive, temper)
    grad_img = for_image(weights, text_low)
    grad_txt = for_text(weights, image_low)
    for text, image in zip(texts, images):
        partner = low_rows(text)
        logits = block_logits(image_low, partner, temper, bias)
        losses = losses + block_losses(logits, negative)
        grad_img = grad_img + for_image(block_weights(logits, negative, temper), partner)
        partner = low_rows(image)
        logits = block_logits(partner, text_low, temper, bias)
        grad_txt = grad_txt + for_text(block_weights(logits, negative, temper), partner)
    grad_image = unit_backward(image_unit, image_scale, grad_img)
    grad_text = unit_backward(text_unit, text_scale, grad_txt)
    return (losses, grad_image, grad_text)


def solution(mesh):
    return jax.shard_map(
        body,
        mesh=mesh,
        in_specs=(P(("blk", "rep"), None), P(("blk", "rep"), None), P(), P()),
        out_specs=(P(("blk", "rep")), P(("blk", "rep"), None), P(("blk", "rep"), None)),
        check_vma=False,
    )
```

```python
import functools

import jax
import jax.numpy as jnp
from jax import lax
from jax.experimental import pallas as pl
from jax.experimental.pallas import tpu as pltpu
from jax.sharding import PartitionSpec as P

AXES = ("blk", "rep")
EPSILON = 1e-06
CHUNK = 256
LANES = 128


def by_role(steps):
    def pairs():
        count = lax.axis_size(AXES)
        return [(b, (b + steps[b % 8]) % count) for b in range(count) if b % 8 in steps]

    return pairs


SWAP = by_role({0: 2, 1: 2, 4: 2, 5: 2, 2: -2, 3: -2, 6: -2, 7: -2})
SECOND = by_role({0: -2, 1: -2, 4: -2, 5: -2, 2: 2, 3: 2, 6: 2, 7: 2})
OF_MAIN = by_role({1: -3, 5: -3, 2: 3, 6: 3, 0: -1, 4: -1, 3: 1, 7: 1})
OF_OTHER = by_role({1: 3, 5: 3, 2: -3, 6: -3, 0: 1, 4: 1, 3: -1, 7: -1})
ON_BY_TWO = by_role({0: -2, 4: -2, 3: 2, 7: 2})
ON_BY_ONE = by_role({0: -1, 4: -1, 3: 1, 7: 1})


def send(x, pairs):
    return lax.ppermute(x, AXES, pairs())


def together(*arrays):
    return lax.optimization_barrier(arrays)


def scale_of(values):
    return lax.rsqrt(jnp.sum(values * values, axis=-1, keepdims=True) + EPSILON)


def lower(raw_ref, low_ref):
    for at in range(0, raw_ref.shape[0], CHUNK):
        rows = pl.ds(at, CHUNK)
        values = raw_ref[rows, :].astype(jnp.float32)
        low_ref[rows, :] = (values * scale_of(values)).astype(jnp.bfloat16)


def terms(logits):
    shrunk = jnp.exp(-jnp.abs(logits))
    total = 1.0 + shrunk
    losses = jnp.maximum(logits, 0.0) + jnp.log(total)
    return losses, jnp.where(logits >= 0.0, 1.0, shrunk) / total


def folded(losses):
    out = losses[:, :LANES]
    for at in range(LANES, losses.shape[1], LANES):
        out = out + losses[:, at : at + LANES]
    return out


def product(left, right, left_dim, right_dim):
    return lax.dot_general(
        left, right, (((left_dim,), (right_dim,)), ((), ())), preferred_element_type=jnp.float32
    )


def pair(numbers_ref, own_ref, partner_ref, acc_ref, loss_ref, counts):
    temper, bias = numbers_ref[0], numbers_ref[1]
    for at in range(0, own_ref.shape[0], CHUNK):
        rows = pl.ds(at, CHUNK)
        logits = temper * product(own_ref[rows, :], partner_ref[...], 1, 1) + bias
        losses, chances = terms(logits)
        loss_ref[rows, :] += counts * folded(losses)
        weights = (chances * temper).astype(jnp.bfloat16)
        acc_ref[rows, :] += product(weights, partner_ref[...], 1, 0)


def finish(raw_ref, acc_ref, out_ref):
    for at in range(0, raw_ref.shape[0], CHUNK):
        rows = pl.ds(at, CHUNK)
        values = raw_ref[rows, :].astype(jnp.float32)
        scale = scale_of(values)
        unit = values * scale
        grad = acc_ref[rows, :]
        out_ref[rows, :] = scale * (grad - unit * jnp.sum(unit * grad, axis=-1, keepdims=True))


def own_pair(numbers_ref, image, text, image_low, text_low, image_acc, text_acc, loss_ref, weights_ref):
    temper, bias = numbers_ref[0], numbers_ref[1]
    lower(image, image_low)
    lower(text, text_low)
    count = image.shape[0]
    for at in range(0, count, CHUNK):
        rows = pl.ds(at, CHUNK)
        logits = temper * product(image_low[rows, :], text_low[...], 1, 1) + bias
        row = lax.broadcasted_iota(jnp.int32, (CHUNK, count), 0) + at
        column = lax.broadcasted_iota(jnp.int32, (CHUNK, count), 1)
        same = row == column
        losses, chances = terms(jnp.where(same, -logits, logits))
        loss_ref[rows, :] = folded(losses)
        weights = (jnp.where(same, -chances, chances) * temper).astype(jnp.bfloat16)
        weights_ref[rows, :] = weights
        image_acc[rows, :] = product(weights, text_low[...], 1, 0)
    text_acc[...] = product(weights_ref[...], image_low[...], 0, 0)


def first_kernel(
    role_ref, numbers_ref, main, other, swapped,
    main_low, other_low, main_acc, other_acc, loss_ref, weights_ref, low_ref,
):
    @pl.when(role_ref[0] == 0)
    def _():
        own_pair(numbers_ref, main, other, main_low, other_low, main_acc, other_acc, loss_ref, weights_ref)

    @pl.when(role_ref[0] == 1)
    def _():
        own_pair(numbers_ref, other, main, other_low, main_low, other_acc, main_acc, loss_ref, weights_ref)

    lower(swapped, low_ref)
    pair(numbers_ref, other_low, low_ref, other_acc, loss_ref, role_ref[0].astype(jnp.float32))


def lower_one_of(chosen, this_ref, that_ref, low_ref):
    @pl.when(chosen)
    def _():
        lower(this_ref, low_ref)

    @pl.when(jnp.logical_not(chosen))
    def _():
        lower(that_ref, low_ref)


def middle_kernel(
    role_ref, numbers_ref, main_low, second, of_main, of_other, main_in, loss_in, main_acc, loss_ref, low_ref
):
    on_main = (1 - role_ref[0]).astype(jnp.float32)
    main_acc[...] = main_in[...]
    loss_ref[...] = loss_in[...]
    for partner in (second, of_main, of_other):
        lower(partner, low_ref)
        pair(numbers_ref, main_low, low_ref, main_acc, loss_ref, on_main)


def put(role_ref, main_side, value_ref, image_out, text_out, sem):
    to_image = role_ref[0] == (0 if main_side else 1)

    @pl.when(to_image)
    def _():
        copy = pltpu.make_async_copy(value_ref, image_out, sem)
        copy.start()
        copy.wait()

    @pl.when(jnp.logical_not(to_image))
    def _():
        copy = pltpu.make_async_copy(value_ref, text_out, sem)
        copy.start()
        copy.wait()


def shared_kernel(
    role_ref, numbers_ref, raw, other_low, swapped, main_in, other_in, loss_in,
    image_out, text_out, other_acc, loss_ref, low_ref, main_acc, sem,
):
    other_acc[...] = other_in[...]
    loss_ref[...] = loss_in[...]
    lower(swapped, low_ref)
    pair(numbers_ref, other_low, low_ref, other_acc, loss_ref, role_ref[0].astype(jnp.float32))
    main_acc[...] = main_in[...]
    finish(raw, main_acc, main_acc)
    put(role_ref, True, main_acc, image_out, text_out, sem)


def last_kernel(
    role_ref, numbers_ref, raw, other_low, by_one, by_two, other_in, loss_in, image_in, text_in,
    image_out, text_out, row_loss, low_ref, other_acc, loss_ref, sem,
):
    on_other = role_ref[0].astype(jnp.float32)
    other_acc[...] = other_in[...]
    loss_ref[...] = loss_in[...]
    lower_one_of(role_ref[0] == role_ref[1], by_one, by_two, low_ref)
    pair(numbers_ref, other_low, low_ref, other_acc, loss_ref, on_other)
    finish(raw, other_acc, other_acc)
    row_loss[...] = jnp.sum(loss_ref[...].T, axis=0, keepdims=True)
    put(role_ref, False, other_acc, image_out, text_out, sem)


def call(kernel, in_kinds, outs, scratch, aliases=None):
    kinds = {
        "s": pl.BlockSpec(memory_space=pltpu.SMEM),
        "v": pl.BlockSpec(memory_space=pltpu.VMEM),
        "a": pl.BlockSpec(memory_space=pl.ANY),
    }
    return pl.pallas_call(
        kernel,
        in_specs=[kinds[k] for k in in_kinds],
        out_specs=[kinds[k] for k, _, _ in outs],
        out_shape=[jax.ShapeDtypeStruct(shape, dtype) for _, shape, dtype in outs],
        scratch_shapes=scratch,
        input_output_aliases=aliases or {},
        compiler_params=pltpu.CompilerParams(vmem_limit_bytes=24 * 1024 * 1024),
    )


def body(image_emb, text_emb, log_temp, bias):
    rows, width = image_emb.shape
    place = lax.axis_index(AXES)
    core = (place // 2) % 2
    role = jnp.stack([core, place % 2]).astype(jnp.int32)
    numbers = jnp.stack([jnp.exp(log_temp), bias])
    is_core_1 = core == 1
    both_or_none = core == place % 2
    main = jnp.where(is_core_1, text_emb, image_emb)
    other = jnp.where(is_core_1, image_emb, text_emb)
    main, other = together(main, other)

    of_other = send(other, OF_OTHER)
    second = send(main, SECOND)
    of_main = send(main, OF_MAIN)
    swapped = send(other, SWAP)

    f32, low = jnp.float32, jnp.bfloat16
    whole, partial = (rows, width), (rows, LANES)
    main_low, other_low, main_acc, other_acc, loss = call(
        first_kernel,
        "ssvvv",
        [("v", whole, low), ("v", whole, low), ("v", whole, f32), ("v", whole, f32), ("v", partial, f32)],
        [pltpu.VMEM((rows, rows), low), pltpu.VMEM(whole, low)],
    )(role, numbers, main, other, swapped)

    of_other, second, of_main, loss = together(of_other, second, of_main, loss)
    by_two = send(of_other, ON_BY_TWO)
    by_one = send(second, ON_BY_ONE)
    swapped = send(jnp.where(both_or_none, of_main, of_other), SWAP)

    main_acc, loss = call(
        middle_kernel,
        "ssvvvvvv",
        [("v", whole, f32), ("v", partial, f32)],
        [pltpu.VMEM(whole, low)],
        {6: 0, 7: 1},
    )(role, numbers, main_low, second, of_main, of_other, main_acc, loss)

    grad_image, grad_text, other_acc, loss = call(
        shared_kernel,
        "ssvvvvvv",
        [("a", whole, f32), ("a", whole, f32), ("v", whole, f32), ("v", partial, f32)],
        [pltpu.VMEM(whole, low), pltpu.VMEM(whole, f32), pltpu.SemaphoreType.DMA],
        {6: 2, 7: 3},
    )(role, numbers, main, other_low, swapped, main_acc, other_acc, loss)

    grad_image, grad_text, row_loss = call(
        last_kernel,
        "ssvvvvvvaa",
        [("a", whole, f32), ("a", whole, f32), ("v", (1, rows), f32)],
        [pltpu.VMEM(whole, low), pltpu.VMEM(whole, f32), pltpu.VMEM(partial, f32), pltpu.SemaphoreType.DMA],
        {8: 0, 9: 1},
    )(role, numbers, other, other_low, by_one, by_two, other_acc, loss, grad_image, grad_text)
    return (row_loss.reshape(rows), grad_image, grad_text)


def solution(mesh):
    return jax.shard_map(
        body,
        mesh=mesh,
        in_specs=(P(AXES, None), P(AXES, None), P(), P()),
        out_specs=(P(AXES), P(AXES, None), P(AXES, None)),
        check_vma=False,
    )
```

```python
import functools

import jax
import jax.numpy as jnp
from jax import lax
from jax.experimental import pallas as pl
from jax.experimental.pallas import tpu as pltpu
from jax.sharding import PartitionSpec as P

AXES = ("blk", "rep")
EPSILON = 1e-06
CHUNK = 256
LANES = 128


def by_role(steps):
    def pairs():
        count = lax.axis_size(AXES)
        return [(b, (b + steps[b % 8]) % count) for b in range(count) if b % 8 in steps]

    return pairs


SWAP = by_role({0: 2, 1: 2, 4: 2, 5: 2, 2: -2, 3: -2, 6: -2, 7: -2})
SECOND = by_role({0: -2, 1: -2, 4: -2, 5: -2, 2: 2, 3: 2, 6: 2, 7: 2})
FAR_OF_MAIN = by_role({1: -3, 5: -3, 2: 3, 6: 3})
NEAR_OF_MAIN = by_role({0: -1, 4: -1, 3: 1, 7: 1})
OF_OTHER = by_role({1: 3, 5: 3, 2: -3, 6: -3, 0: 1, 4: 1, 3: -1, 7: -1})
ON_BY_TWO = by_role({0: -2, 4: -2, 3: 2, 7: 2})
ON_BY_ONE = by_role({0: -1, 4: -1, 3: 1, 7: 1})


def send(x, pairs):
    return lax.ppermute(x, AXES, pairs())


def together(*arrays):
    return lax.optimization_barrier(arrays)


def scale_of(values):
    return lax.rsqrt(jnp.sum(values * values, axis=-1, keepdims=True) + EPSILON)


def lower(raw_ref, low_ref):
    for at in range(0, raw_ref.shape[0], CHUNK):
        rows = pl.ds(at, CHUNK)
        values = raw_ref[rows, :].astype(jnp.float32)
        low_ref[rows, :] = (values * scale_of(values)).astype(jnp.bfloat16)


def terms(logits):
    shrunk = jnp.exp(-jnp.abs(logits))
    total = 1.0 + shrunk
    losses = jnp.maximum(logits, 0.0) + jnp.log(total)
    return losses, jnp.where(logits >= 0.0, 1.0, shrunk) / total


def folded(losses):
    out = losses[:, :LANES]
    for at in range(LANES, losses.shape[1], LANES):
        out = out + losses[:, at : at + LANES]
    return out


def product(left, right, left_dim, right_dim):
    return lax.dot_general(
        left, right, (((left_dim,), (right_dim,)), ((), ())), preferred_element_type=jnp.float32
    )


def partner_grad(numbers_ref, own_ref, partner_ref, loss_from, loss_to, counts, rows):
    temper, bias = numbers_ref[0], numbers_ref[1]
    logits = temper * product(own_ref[rows, :], partner_ref[...], 1, 1) + bias
    losses, chances = terms(logits)
    loss_to[rows, :] = loss_from[rows, :] + counts * folded(losses)
    weights = (chances * temper).astype(jnp.bfloat16)
    return product(weights, partner_ref[...], 1, 0)


def pair(numbers_ref, own_ref, partner_ref, acc_from, acc_to, loss_from, loss_to, counts):
    for at in range(0, own_ref.shape[0], CHUNK):
        rows = pl.ds(at, CHUNK)
        grad = partner_grad(numbers_ref, own_ref, partner_ref, loss_from, loss_to, counts, rows)
        acc_to[rows, :] = acc_from[rows, :] + grad


def closing_pair(
    numbers_ref, raw_ref, own_ref, partner_ref, acc_from, loss_from, loss_to, counts, done_ref, out_ref, sems
):
    copies = []
    for k, at in enumerate(range(0, own_ref.shape[0], CHUNK)):
        rows = pl.ds(at, CHUNK)
        grad = acc_from[rows, :] + partner_grad(
            numbers_ref, own_ref, partner_ref, loss_from, loss_to, counts, rows
        )
        values = raw_ref[rows, :].astype(jnp.float32)
        scale = scale_of(values)
        unit = values * scale
        done_ref[rows, :] = scale * (grad - unit * jnp.sum(unit * grad, axis=-1, keepdims=True))
        copy = pltpu.make_async_copy(done_ref.at[rows, :], out_ref.at[rows, :], sems.at[k])
        copy.start()
        copies.append(copy)
    for copy in copies:
        copy.wait()


def own_pair(numbers_ref, image, text, image_low, text_low, image_acc, text_acc, loss_ref, weights_ref):
    temper, bias = numbers_ref[0], numbers_ref[1]
    lower(image, image_low)
    lower(text, text_low)
    count = image.shape[0]
    for at in range(0, count, CHUNK):
        rows = pl.ds(at, CHUNK)
        logits = temper * product(image_low[rows, :], text_low[...], 1, 1) + bias
        row = lax.broadcasted_iota(jnp.int32, (CHUNK, count), 0) + at
        column = lax.broadcasted_iota(jnp.int32, (CHUNK, count), 1)
        same = row == column
        losses, chances = terms(jnp.where(same, -logits, logits))
        loss_ref[rows, :] = folded(losses)
        weights = (jnp.where(same, -chances, chances) * temper).astype(jnp.bfloat16)
        weights_ref[rows, :] = weights
        image_acc[rows, :] = product(weights, text_low[...], 1, 0)
    text_acc[...] = product(weights_ref[...], image_low[...], 0, 0)


def first_kernel(
    role_ref, numbers_ref, main, other, swapped,
    main_low, other_low, main_acc, other_acc, loss_ref, weights_ref, low_ref,
):
    @pl.when(role_ref[0] == 0)
    def _():
        own_pair(numbers_ref, main, other, main_low, other_low, main_acc, other_acc, loss_ref, weights_ref)

    @pl.when(role_ref[0] == 1)
    def _():
        own_pair(numbers_ref, other, main, other_low, main_low, other_acc, main_acc, loss_ref, weights_ref)

    lower(swapped, low_ref)
    on_other = role_ref[0].astype(jnp.float32)
    pair(numbers_ref, other_low, low_ref, other_acc, other_acc, loss_ref, loss_ref, on_other)


def lower_one_of(chosen, this_ref, that_ref, low_ref):
    @pl.when(chosen)
    def _():
        lower(this_ref, low_ref)

    @pl.when(jnp.logical_not(chosen))
    def _():
        lower(that_ref, low_ref)


def main_kernel(
    role_ref, numbers_ref, main_low, second, near_main, of_other, main_in, loss_in, main_acc, loss_ref, low_ref
):
    on_main = (1 - role_ref[0]).astype(jnp.float32)
    lower(second, low_ref)
    pair(numbers_ref, main_low, low_ref, main_in, main_acc, loss_in, loss_ref, on_main)
    lower_one_of(role_ref[0] == role_ref[1], near_main, of_other, low_ref)
    pair(numbers_ref, main_low, low_ref, main_acc, main_acc, loss_ref, loss_ref, on_main)


def other_kernel(role_ref, numbers_ref, other_low, swapped, other_in, loss_in, other_acc, loss_ref, low_ref):
    lower(swapped, low_ref)
    on_other = role_ref[0].astype(jnp.float32)
    pair(numbers_ref, other_low, low_ref, other_in, other_acc, loss_in, loss_ref, on_other)


def close_sides(
    main_roles_equal, role_ref, numbers_ref, main, other, main_low, other_low, main_acc, other_acc,
    for_main, for_other, loss_in, loss_ref, image_out, text_out, low_ref, done_ref, sems,
):
    core = role_ref[0]
    close_main = (core == role_ref[1]) == main_roles_equal
    lower_one_of(close_main, for_main, for_other, low_ref)
    sides = (
        (close_main, main, main_low, main_acc, 0),
        (jnp.logical_not(close_main), other, other_low, other_acc, 1),
    )
    for chosen, raw, own_low, acc, image_core in sides:
        for at, out, counts in ((image_core, image_out, 1.0), (1 - image_core, text_out, 0.0)):

            @pl.when(jnp.logical_and(chosen, core == at))
            def _(raw=raw, own_low=own_low, acc=acc, out=out, counts=counts):
                closing_pair(
                    numbers_ref, raw, own_low, low_ref, acc, loss_in, loss_ref, counts, done_ref, out, sems
                )


def early_kernel(
    role_ref, numbers_ref, main, other, main_low, other_low, main_acc, other_acc, of_other, by_two, loss_in,
    image_out, text_out, loss_ref, low_ref, done_ref, sems,
):
    close_sides(
        True, role_ref, numbers_ref, main, other, main_low, other_low, main_acc, other_acc,
        of_other, by_two, loss_in, loss_ref, image_out, text_out, low_ref, done_ref, sems,
    )


def late_kernel(
    role_ref, numbers_ref, main, other, main_low, other_low, main_acc, other_acc, far_main, by_one, loss_in,
    image_in, text_in, image_out, text_out, row_loss, low_ref, done_ref, loss_ref, sems,
):
    close_sides(
        False, role_ref, numbers_ref, main, other, main_low, other_low, main_acc, other_acc,
        far_main, by_one, loss_in, loss_ref, image_out, text_out, low_ref, done_ref, sems,
    )
    row_loss[...] = jnp.sum(loss_ref[...].T, axis=0, keepdims=True)


def call(kernel, in_kinds, outs, scratch, aliases=None):
    kinds = {
        "s": pl.BlockSpec(memory_space=pltpu.SMEM),
        "v": pl.BlockSpec(memory_space=pltpu.VMEM),
        "a": pl.BlockSpec(memory_space=pl.ANY),
    }
    return pl.pallas_call(
        kernel,
        in_specs=[kinds[k] for k in in_kinds],
        out_specs=[kinds[k] for k, _, _ in outs],
        out_shape=[jax.ShapeDtypeStruct(shape, dtype) for _, shape, dtype in outs],
        scratch_shapes=scratch,
        input_output_aliases=aliases or {},
        compiler_params=pltpu.CompilerParams(vmem_limit_bytes=24 * 1024 * 1024),
    )


def body(image_emb, text_emb, log_temp, bias):
    rows, width = image_emb.shape
    place = lax.axis_index(AXES)
    core = (place // 2) % 2
    role = jnp.stack([core, place % 2]).astype(jnp.int32)
    numbers = jnp.stack([jnp.exp(log_temp), bias])
    is_core_1 = core == 1
    both_or_none = core == place % 2
    other, image_late, text_late = together(jnp.where(is_core_1, image_emb, text_emb), image_emb, text_emb)
    main = jnp.where(is_core_1, text_late, image_late)

    swapped = send(other, SWAP)
    of_other = send(other, OF_OTHER)
    second = send(main, SECOND)
    near_main = send(main, NEAR_OF_MAIN)

    f32, low = jnp.float32, jnp.bfloat16
    whole, partial = (rows, width), (rows, LANES)
    main_low, other_low, main_acc, other_acc, loss = call(
        first_kernel,
        "ssvvv",
        [("v", whole, low), ("v", whole, low), ("v", whole, f32), ("v", whole, f32), ("v", partial, f32)],
        [pltpu.VMEM((rows, rows), low), pltpu.VMEM(whole, low)],
    )(role, numbers, main, other, swapped)

    of_other, second, near_main, main, loss = together(of_other, second, near_main, main, loss)
    far_main = send(main, FAR_OF_MAIN)
    by_one = send(second, ON_BY_ONE)
    by_two = send(of_other, ON_BY_TWO)
    swapped = send(jnp.where(both_or_none, near_main, of_other), SWAP)

    main_acc, loss = call(
        main_kernel,
        "ssvvvvvv",
        [("v", whole, f32), ("v", partial, f32)],
        [pltpu.VMEM(whole, low)],
        {6: 0, 7: 1},
    )(role, numbers, main_low, second, near_main, of_other, main_acc, loss)
    other_acc, loss = call(
        other_kernel,
        "ssvvvv",
        [("v", whole, f32), ("v", partial, f32)],
        [pltpu.VMEM(whole, low)],
        {4: 0, 5: 1},
    )(role, numbers, other_low, swapped, other_acc, loss)

    sides = (main, other, main_low, other_low, main_acc, other_acc)
    grad_image, grad_text, loss = call(
        early_kernel,
        "ssvvvvvvvvv",
        [("a", whole, f32), ("a", whole, f32), ("v", partial, f32)],
        [pltpu.VMEM(whole, low), pltpu.VMEM(whole, f32), pltpu.SemaphoreType.DMA((rows // CHUNK,))],
        {10: 2},
    )(role, numbers, *sides, of_other, by_two, loss)
    grad_image, grad_text, row_loss = call(
        late_kernel,
        "ssvvvvvvvvvaa",
        [("a", whole, f32), ("a", whole, f32), ("v", (1, rows), f32)],
        [
            pltpu.VMEM(whole, low), pltpu.VMEM(whole, f32), pltpu.VMEM(partial, f32),
            pltpu.SemaphoreType.DMA((rows // CHUNK,)),
        ],
        {11: 0, 12: 1},
    )(role, numbers, *sides, far_main, by_one, loss, grad_image, grad_text)
    return (row_loss.reshape(rows), grad_image, grad_text)


def solution(mesh):
    return jax.shard_map(
        body,
        mesh=mesh,
        in_specs=(P(AXES, None), P(AXES, None), P(), P()),
        out_specs=(P(AXES), P(AXES, None), P(AXES, None)),
        check_vma=False,
    )
```

```python
import functools

import jax
import jax.numpy as jnp
from jax import lax
from jax.experimental import pallas as pl
from jax.experimental.pallas import tpu as pltpu
from jax.sharding import PartitionSpec as P

AXES = ("blk", "rep")
EPSILON = 1e-06
CHUNK = 256
STRIP = 64
LANES = 128


def by_role(steps):
    def pairs():
        count = lax.axis_size(AXES)
        return [(b, (b + steps[b % 8]) % count) for b in range(count) if b % 8 in steps]

    return pairs


SWAP = by_role({0: 2, 1: 2, 4: 2, 5: 2, 2: -2, 3: -2, 6: -2, 7: -2})
SECOND = by_role({0: -2, 1: -2, 4: -2, 5: -2, 2: 2, 3: 2, 6: 2, 7: 2})
OF_OTHER = by_role({1: 3, 5: 3, 2: -3, 6: -3, 0: 1, 4: 1, 3: -1, 7: -1})
NEAR_OF_MAIN = by_role({0: -1, 4: -1, 3: 1, 7: 1})
ON_BY_TWO = by_role({0: -2, 4: -2, 3: 2, 7: 2})
FAR_OR_ON_BY_ONE = by_role({1: -3, 5: -3, 2: 3, 6: 3, 0: -1, 4: -1, 3: 1, 7: 1})


def send(x, pairs):
    return lax.ppermute(x, AXES, pairs())


def together(*arrays):
    return lax.optimization_barrier(arrays)


def strips(count, step):
    def at(k, carry):
        step(pl.ds(pl.multiple_of(k * STRIP, STRIP), STRIP))
        return carry

    lax.fori_loop(0, count // STRIP, at, 0)


def unit_of(raw_ref, rows):
    values = raw_ref[rows, :].astype(jnp.float32)
    scale = lax.rsqrt(jnp.sum(values * values, axis=-1, keepdims=True) + EPSILON)
    return values * scale, scale


def lower(raw_ref, low_ref):
    def step(rows):
        low_ref[rows, :] = unit_of(raw_ref, rows)[0].astype(jnp.bfloat16)

    strips(raw_ref.shape[0], step)


def lower_one_of(chosen, this_ref, that_ref, low_ref):
    @pl.when(chosen)
    def _():
        lower(this_ref, low_ref)

    @pl.when(jnp.logical_not(chosen))
    def _():
        lower(that_ref, low_ref)


def terms(logits):
    shrunk = jnp.exp(-jnp.abs(logits))
    total = 1.0 + shrunk
    losses = jnp.maximum(logits, 0.0) + jnp.log(total)
    return losses, jnp.where(logits >= 0.0, 1.0, shrunk) / total


def folded(losses):
    out = losses[:, :LANES]
    for at in range(LANES, losses.shape[1], LANES):
        out = out + losses[:, at : at + LANES]
    return out


def product(left, right, left_dim, right_dim):
    return lax.dot_general(
        left, right, (((left_dim,), (right_dim,)), ((), ())), preferred_element_type=jnp.float32
    )


def partner_grad(numbers_ref, own_ref, partner_ref, loss_from, loss_to, counts, rows):
    temper, bias = numbers_ref[0], numbers_ref[1]
    logits = temper * product(own_ref[rows, :], partner_ref[...], 1, 1) + bias
    losses, chances = terms(logits)
    loss_to[rows, :] = loss_from[rows, :] + counts * folded(losses)
    weights = (chances * temper).astype(jnp.bfloat16)
    return product(weights, partner_ref[...], 1, 0)


def pair(numbers_ref, own_ref, partner_ref, acc_from, acc_to, loss_from, loss_to, counts):
    for at in range(0, own_ref.shape[0], CHUNK):
        rows = pl.ds(at, CHUNK)
        grad = partner_grad(numbers_ref, own_ref, partner_ref, loss_from, loss_to, counts, rows)
        acc_to[rows, :] = acc_from[rows, :] + grad


def first_kernel(
    role_ref, numbers_ref, main, other, swapped,
    lows, units, scales, accs, loss_ref, weights_ref, low_ref,
):
    temper, bias = numbers_ref[0], numbers_ref[1]
    core = role_ref[0]
    count = main.shape[0]
    for side, raw in enumerate((main, other)):

        def step(rows, side=side, raw=raw):
            unit, scale = unit_of(raw, rows)
            units[side, rows, :] = unit
            scales[side, rows, :] = scale
            lows[side, rows, :] = unit.astype(jnp.bfloat16)

        strips(count, step)
    image_low, text_low = lows.at[core], lows.at[1 - core]
    for at in range(0, count, CHUNK):
        rows = pl.ds(at, CHUNK)
        logits = temper * product(image_low[rows, :], text_low[...], 1, 1) + bias
        row = lax.broadcasted_iota(jnp.int32, (CHUNK, count), 0) + at
        column = lax.broadcasted_iota(jnp.int32, (CHUNK, count), 1)
        same = row == column
        losses, chances = terms(jnp.where(same, -logits, logits))
        loss_ref[rows, :] = folded(losses)
        weights = (jnp.where(same, -chances, chances) * temper).astype(jnp.bfloat16)
        weights_ref[rows, :] = weights
        accs[core, rows, :] = product(weights, text_low[...], 1, 0)
    accs[1 - core] = product(weights_ref[...], image_low[...], 0, 0)
    lower(swapped, low_ref)
    pair(
        numbers_ref, lows.at[1], low_ref, accs.at[1], accs.at[1], loss_ref, loss_ref, core.astype(jnp.float32)
    )


def sent_kernel(role_ref, lows, second, near_main, of_other, near_low, late_low):
    outer = role_ref[0] == role_ref[1]
    lower_one_of(outer, near_main, of_other, near_low)

    @pl.when(outer)
    def _():
        lower(second, late_low)

    @pl.when(jnp.logical_not(outer))
    def _():
        late_low[...] = lows[0]


def middle_kernel(
    role_ref, numbers_ref, lows, second, near_low, swapped, accs_in, loss_in, accs, loss_ref, low_ref
):
    on_other = role_ref[0].astype(jnp.float32)
    on_main = 1.0 - on_other
    pair(numbers_ref, lows.at[0], near_low, accs_in.at[0], accs.at[0], loss_in, loss_ref, on_main)
    lower(second, low_ref)
    pair(numbers_ref, lows.at[0], low_ref, accs.at[0], accs.at[0], loss_ref, loss_ref, on_main)
    pair(numbers_ref, lows.at[1], swapped, accs_in.at[1], accs.at[1], loss_ref, loss_ref, on_other)


def close_side(
    side, core, numbers_ref, lows, units, scales, accs, partner_ref, loss_from, loss_to,
    image_out, text_out, done_ref, sems,
):
    counts = (side == core).astype(jnp.float32)
    own_low = lows.at[side]

    parts = done_ref.shape[0] // CHUNK

    def copy(k, out):
        rows = pl.ds(k * CHUNK, CHUNK)
        return pltpu.make_async_copy(done_ref.at[rows, :], out.at[rows, :], sems.at[k])

    for k in range(parts):
        rows = pl.ds(k * CHUNK, CHUNK)
        grad = accs[side, rows, :] + partner_grad(
            numbers_ref, own_low, partner_ref, loss_from, loss_to, counts, rows
        )
        unit = units[side, rows, :]
        along = jnp.sum(unit * grad, axis=-1, keepdims=True)
        done_ref[rows, :] = scales[side, rows, :] * (grad - unit * along)

        @pl.when(side == core)
        def _():
            copy(k, image_out).start()

        @pl.when(side != core)
        def _():
            copy(k, text_out).start()

    @pl.when(side == core)
    def _():
        for k in range(parts):
            copy(k, image_out).wait()

    @pl.when(side != core)
    def _():
        for k in range(parts):
            copy(k, text_out).wait()


def early_kernel(
    role_ref, numbers_ref, lows, units, scales, accs, of_other, by_two, loss_in,
    image_out, text_out, loss_ref, low_ref, done_ref, sems,
):
    outer = role_ref[0] == role_ref[1]
    lower_one_of(outer, of_other, by_two, low_ref)
    close_side(
        jnp.where(outer, 0, 1), role_ref[0], numbers_ref, lows, units, scales, accs, low_ref,
        loss_in, loss_ref, image_out, text_out, done_ref, sems,
    )


def late_kernel(
    role_ref, numbers_ref, lows, units, scales, accs, late_low, loss_in, image_in, text_in,
    image_out, text_out, row_loss, loss_ref, done_ref, sems,
):
    outer = role_ref[0] == role_ref[1]
    close_side(
        jnp.where(outer, 1, 0), role_ref[0], numbers_ref, lows, units, scales, accs, late_low,
        loss_in, loss_ref, image_out, text_out, done_ref, sems,
    )
    row_loss[...] = jnp.sum(loss_ref[...].T, axis=0, keepdims=True)


def call(kernel, in_kinds, outs, scratch=(), aliases=None):
    kinds = {
        "s": pl.BlockSpec(memory_space=pltpu.SMEM),
        "v": pl.BlockSpec(memory_space=pltpu.VMEM),
        "a": pl.BlockSpec(memory_space=pl.ANY),
    }
    return pl.pallas_call(
        kernel,
        in_specs=[kinds[k] for k in in_kinds],
        out_specs=[kinds[k] for k, _, _ in outs],
        out_shape=[jax.ShapeDtypeStruct(shape, dtype) for _, shape, dtype in outs],
        scratch_shapes=list(scratch),
        input_output_aliases=aliases or {},
        compiler_params=pltpu.CompilerParams(vmem_limit_bytes=24 * 1024 * 1024),
    )


def body(image_emb, text_emb, log_temp, bias):
    rows, width = image_emb.shape
    place = lax.axis_index(AXES)
    core = (place // 2) % 2
    role = jnp.stack([core, place % 2]).astype(jnp.int32)
    numbers = jnp.stack([jnp.exp(log_temp), bias])
    is_core_1 = core == 1
    other, image_late, text_late = together(jnp.where(is_core_1, image_emb, text_emb), image_emb, text_emb)
    main = jnp.where(is_core_1, text_late, image_late)

    swapped = send(other, SWAP)
    of_other = send(other, OF_OTHER)
    second = send(main, SECOND)
    near_main = send(main, NEAR_OF_MAIN)

    f32, low = jnp.float32, jnp.bfloat16
    whole, partial, both = (rows, width), (rows, LANES), (2, rows, width)
    lows, units, scales, accs, loss = call(
        first_kernel,
        "ssvvv",
        [("v", both, low), ("v", both, f32), ("v", (2, rows, 1), f32), ("v", both, f32), ("v", partial, f32)],
        [pltpu.VMEM((rows, rows), low), pltpu.VMEM(whole, low)],
    )(role, numbers, main, other, swapped)

    of_other, second, near_main, loss = together(of_other, second, near_main, loss)
    by_two = send(of_other, ON_BY_TWO)
    near_low, late_low = call(sent_kernel, "svvvv", [("v", whole, low), ("v", whole, low)])(
        role, lows, second, near_main, of_other
    )
    late_low = send(late_low, FAR_OR_ON_BY_ONE)
    swapped = send(near_low, SWAP)

    accs, loss = call(
        middle_kernel,
        "ssvvvvvv",
        [("v", both, f32), ("v", partial, f32)],
        [pltpu.VMEM(whole, low)],
        {6: 0, 7: 1},
    )(role, numbers, lows, second, near_low, swapped, accs, loss)

    copy_sems = pltpu.SemaphoreType.DMA((rows // CHUNK,))
    grad_image, grad_text, loss = call(
        early_kernel,
        "ssvvvvvvv",
        [("a", whole, f32), ("a", whole, f32), ("v", partial, f32)],
        [pltpu.VMEM(whole, low), pltpu.VMEM(whole, f32), copy_sems],
        {8: 2},
    )(role, numbers, lows, units, scales, accs, of_other, by_two, loss)
    grad_image, grad_text, row_loss = call(
        late_kernel,
        "ssvvvvvvaa",
        [("a", whole, f32), ("a", whole, f32), ("v", (1, rows), f32)],
        [pltpu.VMEM(partial, f32), pltpu.VMEM(whole, f32), copy_sems],
        {8: 0, 9: 1},
    )(role, numbers, lows, units, scales, accs, late_low, loss, grad_image, grad_text)
    return (row_loss.reshape(rows), grad_image, grad_text)


def solution(mesh):
    return jax.shard_map(
        body,
        mesh=mesh,
        in_specs=(P(AXES, None), P(AXES, None), P(), P()),
        out_specs=(P(AXES), P(AXES, None), P(AXES, None)),
        check_vma=False,
    )
```

```python
import functools

import jax
import jax.numpy as jnp
from jax import lax
from jax.experimental import pallas as pl
from jax.experimental.pallas import tpu as pltpu
from jax.sharding import PartitionSpec as P

AXES = ("blk", "rep")
EPSILON = 1e-06
COLUMNS = 512
STRIP = 512
LANES = 128


def by_role(steps):
    def pairs():
        count = lax.axis_size(AXES)
        return [(b, (b + steps[b % 8]) % count) for b in range(count) if b % 8 in steps]

    return pairs


SWAP = by_role({0: 2, 1: 2, 4: 2, 5: 2, 2: -2, 3: -2, 6: -2, 7: -2})
SECOND = by_role({0: -2, 1: -2, 4: -2, 5: -2, 2: 2, 3: 2, 6: 2, 7: 2})
OF_OTHER = by_role({1: 3, 5: 3, 2: -3, 6: -3, 0: 1, 4: 1, 3: -1, 7: -1})
NEAR_OF_MAIN = by_role({0: -1, 4: -1, 3: 1, 7: 1})
ON_BY_TWO = by_role({0: -2, 4: -2, 3: 2, 7: 2})
FAR_OR_ON_BY_ONE = by_role({1: -3, 5: -3, 2: 3, 6: 3, 0: -1, 4: -1, 3: 1, 7: 1})


def send(x, pairs):
    return lax.ppermute(x, AXES, pairs())


def together(*arrays):
    return lax.optimization_barrier(arrays)


def unit_of(raw_ref, rows):
    values = raw_ref[rows, :].astype(jnp.float32)
    scale = lax.rsqrt(jnp.sum(values * values, axis=-1, keepdims=True) + EPSILON)
    return values * scale, scale


def lower(raw_ref, low_ref):
    low_ref[...] = unit_of(raw_ref, slice(None))[0].astype(jnp.bfloat16)


def lower_one_of(chosen, this_ref, that_ref, low_ref):
    @pl.when(chosen)
    def _():
        lower(this_ref, low_ref)

    @pl.when(jnp.logical_not(chosen))
    def _():
        lower(that_ref, low_ref)


def terms(logits):
    shrunk = jnp.exp(-jnp.abs(logits))
    total = 1.0 + shrunk
    losses = jnp.maximum(logits, 0.0) + jnp.log(total)
    return losses, jnp.where(logits >= 0.0, 1.0, shrunk) / total


def folded(losses):
    out = losses[:, :LANES]
    for at in range(LANES, losses.shape[1], LANES):
        out = out + losses[:, at : at + LANES]
    return out


def product(left, right, left_dim, right_dim):
    return lax.dot_general(
        left, right, (((left_dim,), (right_dim,)), ((), ())), preferred_element_type=jnp.float32
    )


def partner_grad(numbers_ref, own_ref, partner_ref, loss_from, loss_to, counts):
    temper, bias = numbers_ref[0], numbers_ref[1]
    loss, grad = 0.0, 0.0
    for at in range(0, partner_ref.shape[0], COLUMNS):
        partner = partner_ref[pl.ds(at, COLUMNS), :]
        losses, chances = terms(temper * product(own_ref[...], partner, 1, 1) + bias)
        loss = loss + folded(losses)
        grad = grad + product((chances * temper).astype(jnp.bfloat16), partner, 1, 0)
    loss_to[...] = loss_from[...] + counts * loss
    return grad


def pair(numbers_ref, own_ref, partner_ref, acc_from, acc_to, loss_from, loss_to, counts):
    acc_to[...] = acc_from[...] + partner_grad(
        numbers_ref, own_ref, partner_ref, loss_from, loss_to, counts
    )


def first_kernel(
    role_ref, numbers_ref, main, other, swapped,
    lows, units, scales, accs, loss_ref, weights_ref, low_ref,
):
    temper, bias = numbers_ref[0], numbers_ref[1]
    core = role_ref[0]
    count = main.shape[0]
    for side, raw in enumerate((main, other)):
        unit, scale = unit_of(raw, slice(None))
        units[side] = unit
        scales[side] = scale
        lows[side] = unit.astype(jnp.bfloat16)
    image_low, text_low = lows.at[core], lows.at[1 - core]
    logits = temper * product(image_low[...], text_low[...], 1, 1) + bias
    row = lax.broadcasted_iota(jnp.int32, (count, count), 0)
    column = lax.broadcasted_iota(jnp.int32, (count, count), 1)
    same = row == column
    losses, chances = terms(jnp.where(same, -logits, logits))
    loss_ref[...] = folded(losses)
    weights = (jnp.where(same, -chances, chances) * temper).astype(jnp.bfloat16)
    weights_ref[...] = weights
    accs[core] = product(weights, text_low[...], 1, 0)
    accs[1 - core] = product(weights_ref[...], image_low[...], 0, 0)
    lower(swapped, low_ref)
    pair(
        numbers_ref, lows.at[1], low_ref, accs.at[1], accs.at[1], loss_ref, loss_ref, core.astype(jnp.float32)
    )


def sent_kernel(role_ref, lows, second, near_main, of_other, near_low, late_low):
    outer = role_ref[0] == role_ref[1]
    lower_one_of(outer, near_main, of_other, near_low)

    @pl.when(outer)
    def _():
        lower(second, late_low)

    @pl.when(jnp.logical_not(outer))
    def _():
        late_low[...] = lows[0]


def middle_kernel(
    role_ref, numbers_ref, lows, second, near_low, swapped, accs_in, loss_in, accs, loss_ref, low_ref
):
    on_other = role_ref[0].astype(jnp.float32)
    on_main = 1.0 - on_other
    pair(numbers_ref, lows.at[0], near_low, accs_in.at[0], accs.at[0], loss_in, loss_ref, on_main)
    lower(second, low_ref)
    pair(numbers_ref, lows.at[0], low_ref, accs.at[0], accs.at[0], loss_ref, loss_ref, on_main)
    pair(numbers_ref, lows.at[1], swapped, accs_in.at[1], accs.at[1], loss_ref, loss_ref, on_other)


def close_side(
    side, core, numbers_ref, lows, units, scales, accs, partner_ref, loss_from, loss_to,
    image_out, text_out, done_ref, sems,
):
    counts = (side == core).astype(jnp.float32)
    own_low = lows.at[side]

    parts = done_ref.shape[0] // STRIP

    def copy(k, out):
        rows = pl.ds(k * STRIP, STRIP)
        return pltpu.make_async_copy(done_ref.at[rows, :], out.at[rows, :], sems.at[k])

    done_ref[...] = accs[side] + partner_grad(numbers_ref, own_low, partner_ref, loss_from, loss_to, counts)
    for k in range(parts):
        rows = pl.ds(k * STRIP, STRIP)
        grad = done_ref[rows, :]
        unit = units[side, rows, :]
        along = jnp.sum(unit * grad, axis=-1, keepdims=True)
        done_ref[rows, :] = scales[side, rows, :] * (grad - unit * along)

        @pl.when(side == core)
        def _():
            copy(k, image_out).start()

        @pl.when(side != core)
        def _():
            copy(k, text_out).start()

    @pl.when(side == core)
    def _():
        for k in range(parts):
            copy(k, image_out).wait()

    @pl.when(side != core)
    def _():
        for k in range(parts):
            copy(k, text_out).wait()


def early_kernel(
    role_ref, numbers_ref, lows, units, scales, accs, of_other, by_two, loss_in,
    image_out, text_out, loss_ref, low_ref, done_ref, sems,
):
    outer = role_ref[0] == role_ref[1]
    lower_one_of(outer, of_other, by_two, low_ref)
    close_side(
        jnp.where(outer, 0, 1), role_ref[0], numbers_ref, lows, units, scales, accs, low_ref,
        loss_in, loss_ref, image_out, text_out, done_ref, sems,
    )


def late_kernel(
    role_ref, numbers_ref, lows, units, scales, accs, late_low, loss_in, image_in, text_in,
    image_out, text_out, row_loss, loss_ref, done_ref, sems,
):
    outer = role_ref[0] == role_ref[1]
    close_side(
        jnp.where(outer, 1, 0), role_ref[0], numbers_ref, lows, units, scales, accs, late_low,
        loss_in, loss_ref, image_out, text_out, done_ref, sems,
    )
    row_loss[...] = jnp.sum(loss_ref[...].T, axis=0, keepdims=True)


def call(kernel, in_kinds, outs, scratch=(), aliases=None):
    kinds = {
        "s": pl.BlockSpec(memory_space=pltpu.SMEM),
        "v": pl.BlockSpec(memory_space=pltpu.VMEM),
        "a": pl.BlockSpec(memory_space=pl.ANY),
    }
    return pl.pallas_call(
        kernel,
        in_specs=[kinds[k] for k in in_kinds],
        out_specs=[kinds[k] for k, _, _ in outs],
        out_shape=[jax.ShapeDtypeStruct(shape, dtype) for _, shape, dtype in outs],
        scratch_shapes=list(scratch),
        input_output_aliases=aliases or {},
        compiler_params=pltpu.CompilerParams(vmem_limit_bytes=24 * 1024 * 1024),
    )


def body(image_emb, text_emb, log_temp, bias):
    rows, width = image_emb.shape
    place = lax.axis_index(AXES)
    core = (place // 2) % 2
    role = jnp.stack([core, place % 2]).astype(jnp.int32)
    numbers = jnp.stack([jnp.exp(log_temp), bias])
    is_core_1 = core == 1
    other, image_late, text_late = together(jnp.where(is_core_1, image_emb, text_emb), image_emb, text_emb)
    main = jnp.where(is_core_1, text_late, image_late)

    swapped = send(other, SWAP)
    of_other = send(other, OF_OTHER)
    second = send(main, SECOND)
    near_main = send(main, NEAR_OF_MAIN)

    f32, low = jnp.float32, jnp.bfloat16
    whole, partial, both = (rows, width), (rows, LANES), (2, rows, width)
    lows, units, scales, accs, loss = call(
        first_kernel,
        "ssvvv",
        [("v", both, low), ("v", both, f32), ("v", (2, rows, 1), f32), ("v", both, f32), ("v", partial, f32)],
        [pltpu.VMEM((rows, rows), low), pltpu.VMEM(whole, low)],
    )(role, numbers, main, other, swapped)

    near_main, second, of_other, loss = together(near_main, second, of_other, loss)
    by_two = send(of_other, ON_BY_TWO)
    near_low, late_low = call(sent_kernel, "svvvv", [("v", whole, low), ("v", whole, low)])(
        role, lows, second, near_main, of_other
    )
    late_low = send(late_low, FAR_OR_ON_BY_ONE)
    swapped = send(near_low, SWAP)

    accs, loss = call(
        middle_kernel,
        "ssvvvvvv",
        [("v", both, f32), ("v", partial, f32)],
        [pltpu.VMEM(whole, low)],
        {6: 0, 7: 1},
    )(role, numbers, lows, second, near_low, swapped, accs, loss)

    copy_sems = pltpu.SemaphoreType.DMA((rows // STRIP,))
    grad_image, grad_text, loss = call(
        early_kernel,
        "ssvvvvvvv",
        [("a", whole, f32), ("a", whole, f32), ("v", partial, f32)],
        [pltpu.VMEM(whole, low), pltpu.VMEM(whole, f32), copy_sems],
        {8: 2},
    )(role, numbers, lows, units, scales, accs, of_other, by_two, loss)
    grad_image, grad_text, row_loss = call(
        late_kernel,
        "ssvvvvvvaa",
        [("a", whole, f32), ("a", whole, f32), ("v", (1, rows), f32)],
        [pltpu.VMEM(partial, f32), pltpu.VMEM(whole, f32), copy_sems],
        {8: 0, 9: 1},
    )(role, numbers, lows, units, scales, accs, late_low, loss, grad_image, grad_text)
    return (row_loss.reshape(rows), grad_image, grad_text)


def solution(mesh):
    return jax.shard_map(
        body,
        mesh=mesh,
        in_specs=(P(AXES, None), P(AXES, None), P(), P()),
        out_specs=(P(AXES), P(AXES, None), P(AXES, None)),
        check_vma=False,
    )
```

```python
import functools

import jax
import jax.numpy as jnp
from jax import lax
from jax.experimental import pallas as pl
from jax.experimental.pallas import tpu as pltpu
from jax.sharding import PartitionSpec as P

AXES = ("blk", "rep")
EPSILON = 1e-06
COLUMNS = 512
STRIP = 512
LANES = 128


def by_role(steps):
    def pairs():
        count = lax.axis_size(AXES)
        return [(b, (b + steps[b % 8]) % count) for b in range(count) if b % 8 in steps]

    return pairs


SWAP = by_role({0: 2, 1: 2, 4: 2, 5: 2, 2: -2, 3: -2, 6: -2, 7: -2})
SECOND = by_role({0: -2, 1: -2, 4: -2, 5: -2, 2: 2, 3: 2, 6: 2, 7: 2})
OF_OTHER = by_role({1: 3, 5: 3, 2: -3, 6: -3, 0: 1, 4: 1, 3: -1, 7: -1})
NEAR_OF_MAIN = by_role({0: -1, 4: -1, 3: 1, 7: 1})
ON_BY_TWO = by_role({0: -2, 4: -2, 3: 2, 7: 2})
FAR_OR_ON_BY_ONE = by_role({1: -3, 5: -3, 2: 3, 6: 3, 0: -1, 4: -1, 3: 1, 7: 1})


def send(x, pairs):
    return lax.ppermute(x, AXES, pairs())


def together(*arrays):
    return lax.optimization_barrier(arrays)


def unit_of(raw_ref, rows):
    values = raw_ref[rows, :].astype(jnp.float32)
    scale = lax.rsqrt(jnp.sum(values * values, axis=-1, keepdims=True) + EPSILON)
    return values * scale, scale


def lower(raw_ref, low_ref):
    low_ref[...] = unit_of(raw_ref, slice(None))[0].astype(jnp.bfloat16)


def lower_one_of(chosen, this_ref, that_ref, low_ref):
    @pl.when(chosen)
    def _():
        lower(this_ref, low_ref)

    @pl.when(jnp.logical_not(chosen))
    def _():
        lower(that_ref, low_ref)


def terms(logits):
    shrunk = jnp.exp(-jnp.abs(logits))
    total = 1.0 + shrunk
    losses = jnp.maximum(logits, 0.0) + jnp.log(total)
    return losses, jnp.where(logits >= 0.0, 1.0, shrunk) / total


def folded(losses):
    out = losses[:, :LANES]
    for at in range(LANES, losses.shape[1], LANES):
        out = out + losses[:, at : at + LANES]
    return out


def product(left, right, left_dim, right_dim):
    return lax.dot_general(
        left, right, (((left_dim,), (right_dim,)), ((), ())), preferred_element_type=jnp.float32
    )


def partner_grad(numbers_ref, own_ref, partner_ref, loss_from, loss_to, counts):
    temper, bias = numbers_ref[0], numbers_ref[1]
    loss, grad = 0.0, 0.0
    for at in range(0, partner_ref.shape[0], COLUMNS):
        partner = partner_ref[pl.ds(at, COLUMNS), :]
        losses, chances = terms(temper * product(own_ref[...], partner, 1, 1) + bias)
        loss = loss + folded(losses)
        grad = grad + product((chances * temper).astype(jnp.bfloat16), partner, 1, 0)
    loss_to[...] = loss_from[...] + counts * loss
    return grad


def pair(numbers_ref, own_ref, partner_ref, acc_from, acc_to, loss_from, loss_to, counts):
    acc_to[...] = acc_from[...] + partner_grad(
        numbers_ref, own_ref, partner_ref, loss_from, loss_to, counts
    )


def first_kernel(
    role_ref, numbers_ref, main, other, swapped,
    lows, units, scales, accs, loss_ref, weights_ref, low_ref,
):
    temper, bias = numbers_ref[0], numbers_ref[1]
    core = role_ref[0]
    count = main.shape[0]
    for side, raw in enumerate((main, other)):
        unit, scale = unit_of(raw, slice(None))
        units[side] = unit
        scales[side] = scale
        lows[side] = unit.astype(jnp.bfloat16)
    image_low, text_low = lows.at[core], lows.at[1 - core]
    logits = temper * product(image_low[...], text_low[...], 1, 1) + bias
    row = lax.broadcasted_iota(jnp.int32, (count, count), 0)
    column = lax.broadcasted_iota(jnp.int32, (count, count), 1)
    same = row == column
    losses, chances = terms(jnp.where(same, -logits, logits))
    loss_ref[...] = folded(losses)
    weights = (jnp.where(same, -chances, chances) * temper).astype(jnp.bfloat16)
    weights_ref[...] = weights
    accs[core] = product(weights, text_low[...], 1, 0)
    accs[1 - core] = product(weights_ref[...], image_low[...], 0, 0)
    lower(swapped, low_ref)
    pair(
        numbers_ref, lows.at[1], low_ref, accs.at[1], accs.at[1], loss_ref, loss_ref, core.astype(jnp.float32)
    )


def sent_kernel(role_ref, lows, second, near_main, of_other, near_low, late_low):
    outer = role_ref[0] == role_ref[1]
    lower_one_of(outer, near_main, of_other, near_low)

    @pl.when(outer)
    def _():
        lower(second, late_low)

    @pl.when(jnp.logical_not(outer))
    def _():
        late_low[...] = lows[0]


def middle_kernel(
    role_ref, numbers_ref, lows, second, near_low, swapped, accs_in, loss_in, accs, loss_ref, low_ref
):
    on_other = role_ref[0].astype(jnp.float32)
    on_main = 1.0 - on_other
    pair(numbers_ref, lows.at[0], near_low, accs_in.at[0], accs.at[0], loss_in, loss_ref, on_main)
    lower(second, low_ref)
    pair(numbers_ref, lows.at[0], low_ref, accs.at[0], accs.at[0], loss_ref, loss_ref, on_main)
    pair(numbers_ref, lows.at[1], swapped, accs_in.at[1], accs.at[1], loss_ref, loss_ref, on_other)


def close_side(
    side, core, numbers_ref, lows, units, scales, accs, partner_ref, loss_from, loss_to,
    image_out, text_out, done_ref, sems,
):
    counts = (side == core).astype(jnp.float32)
    own_low = lows.at[side]

    parts = done_ref.shape[0] // STRIP

    def copy(k, out):
        rows = pl.ds(k * STRIP, STRIP)
        return pltpu.make_async_copy(done_ref.at[rows, :], out.at[rows, :], sems.at[k])

    done_ref[...] = accs[side] + partner_grad(numbers_ref, own_low, partner_ref, loss_from, loss_to, counts)
    for k in range(parts):
        rows = pl.ds(k * STRIP, STRIP)
        grad = done_ref[rows, :]
        unit = units[side, rows, :]
        along = jnp.sum(unit * grad, axis=-1, keepdims=True)
        done_ref[rows, :] = scales[side, rows, :] * (grad - unit * along)

        @pl.when(side == core)
        def _():
            copy(k, image_out).start()

        @pl.when(side != core)
        def _():
            copy(k, text_out).start()

    @pl.when(side == core)
    def _():
        for k in range(parts):
            copy(k, image_out).wait()

    @pl.when(side != core)
    def _():
        for k in range(parts):
            copy(k, text_out).wait()


def early_kernel(
    role_ref, numbers_ref, lows, units, scales, accs, of_other, by_two, loss_in,
    image_out, text_out, loss_ref, low_ref, done_ref, sems,
):
    outer = role_ref[0] == role_ref[1]
    lower_one_of(outer, of_other, by_two, low_ref)
    close_side(
        jnp.where(outer, 0, 1), role_ref[0], numbers_ref, lows, units, scales, accs, low_ref,
        loss_in, loss_ref, image_out, text_out, done_ref, sems,
    )


def late_kernel(
    role_ref, numbers_ref, lows, units, scales, accs, late_low, loss_in, image_in, text_in,
    image_out, text_out, row_loss, loss_ref, done_ref, sems,
):
    outer = role_ref[0] == role_ref[1]
    close_side(
        jnp.where(outer, 1, 0), role_ref[0], numbers_ref, lows, units, scales, accs, late_low,
        loss_in, loss_ref, image_out, text_out, done_ref, sems,
    )
    row_loss[...] = jnp.sum(loss_ref[...].T, axis=0, keepdims=True)


def call(kernel, in_kinds, outs, scratch=(), aliases=None):
    kinds = {
        "s": pl.BlockSpec(memory_space=pltpu.SMEM),
        "v": pl.BlockSpec(memory_space=pltpu.VMEM),
        "a": pl.BlockSpec(memory_space=pl.ANY),
    }
    return pl.pallas_call(
        kernel,
        in_specs=[kinds[k] for k in in_kinds],
        out_specs=[kinds[k] for k, _, _ in outs],
        out_shape=[jax.ShapeDtypeStruct(shape, dtype) for _, shape, dtype in outs],
        scratch_shapes=list(scratch),
        input_output_aliases=aliases or {},
        compiler_params=pltpu.CompilerParams(vmem_limit_bytes=24 * 1024 * 1024),
    )


def body(image_emb, text_emb, log_temp, bias):
    rows, width = image_emb.shape
    place = lax.axis_index(AXES)
    core = (place // 2) % 2
    role = jnp.stack([core, place % 2]).astype(jnp.int32)
    numbers = jnp.stack([jnp.exp(log_temp), bias])
    is_core_1 = core == 1
    other, image_late, text_late = together(jnp.where(is_core_1, image_emb, text_emb), image_emb, text_emb)
    main = jnp.where(is_core_1, text_late, image_late)

    swapped = send(other, SWAP)
    of_other = send(other, OF_OTHER)
    second = send(main, SECOND)
    near_main = send(main, NEAR_OF_MAIN)

    f32, low = jnp.float32, jnp.bfloat16
    whole, partial, both = (rows, width), (rows, LANES), (2, rows, width)
    lows, units, scales, accs, loss = call(
        first_kernel,
        "ssvvv",
        [("v", both, low), ("v", both, f32), ("v", (2, rows, 1), f32), ("v", both, f32), ("v", partial, f32)],
        [pltpu.VMEM((rows, rows), low), pltpu.VMEM(whole, low)],
    )(role, numbers, main, other, swapped)

    of_other, second, near_main, loss = together(of_other, second, near_main, loss)
    by_two = send(of_other, ON_BY_TWO)
    near_low, late_low = call(sent_kernel, "svvvv", [("v", whole, low), ("v", whole, low)])(
        role, lows, second, near_main, of_other
    )
    late_low = send(late_low, FAR_OR_ON_BY_ONE)
    swapped = send(near_low, SWAP)

    accs, loss = call(
        middle_kernel,
        "ssvvvvvv",
        [("v", both, f32), ("v", partial, f32)],
        [pltpu.VMEM(whole, low)],
        {6: 0, 7: 1},
    )(role, numbers, lows, second, near_low, swapped, accs, loss)

    copy_sems = pltpu.SemaphoreType.DMA((rows // STRIP,))
    grad_image, grad_text, loss = call(
        early_kernel,
        "ssvvvvvvv",
        [("a", whole, f32), ("a", whole, f32), ("v", partial, f32)],
        [pltpu.VMEM(whole, low), pltpu.VMEM(whole, f32), copy_sems],
        {8: 2},
    )(role, numbers, lows, units, scales, accs, of_other, by_two, loss)
    grad_image, grad_text, row_loss = call(
        late_kernel,
        "ssvvvvvvaa",
        [("a", whole, f32), ("a", whole, f32), ("v", (1, rows), f32)],
        [pltpu.VMEM(partial, f32), pltpu.VMEM(whole, f32), copy_sems],
        {8: 0, 9: 1},
    )(role, numbers, lows, units, scales, accs, late_low, loss, grad_image, grad_text)
    return (row_loss.reshape(rows), grad_image, grad_text)


def solution(mesh):
    return jax.shard_map(
        body,
        mesh=mesh,
        in_specs=(P(AXES, None), P(AXES, None), P(), P()),
        out_specs=(P(AXES), P(AXES, None), P(AXES, None)),
        check_vma=False,
    )
```

```python
import functools

import jax
import jax.numpy as jnp
from jax import lax
from jax.experimental import pallas as pl
from jax.experimental.pallas import tpu as pltpu
from jax.sharding import PartitionSpec as P

AXES = ("blk", "rep")
EPSILON = 1e-06
COLUMNS = 512
STRIP = 512
LANES = 128


def by_role(steps):
    def pairs():
        count = lax.axis_size(AXES)
        return [(b, (b + steps[b % 8]) % count) for b in range(count) if b % 8 in steps]

    return pairs


SWAP = by_role({0: 2, 1: 2, 4: 2, 5: 2, 2: -2, 3: -2, 6: -2, 7: -2})
SECOND = by_role({0: -2, 1: -2, 4: -2, 5: -2, 2: 2, 3: 2, 6: 2, 7: 2})
OF_OTHER = by_role({1: 3, 5: 3, 2: -3, 6: -3, 0: 1, 4: 1, 3: -1, 7: -1})
NEAR_OF_MAIN = by_role({0: -1, 4: -1, 3: 1, 7: 1})
ON_BY_TWO = by_role({0: -2, 4: -2, 3: 2, 7: 2})
FAR_OR_ON_BY_ONE = by_role({1: -3, 5: -3, 2: 3, 6: 3, 0: -1, 4: -1, 3: 1, 7: 1})


def send(x, pairs):
    return lax.ppermute(x, AXES, pairs())


def together(*arrays):
    return lax.optimization_barrier(arrays)


def unit_of(raw_ref, rows):
    values = raw_ref[rows, :].astype(jnp.float32)
    scale = lax.rsqrt(jnp.sum(values * values, axis=-1, keepdims=True) + EPSILON)
    return values * scale, scale


def lower(raw_ref, low_ref):
    low_ref[...] = unit_of(raw_ref, slice(None))[0].astype(jnp.bfloat16)


def lower_one_of(chosen, this_ref, that_ref, low_ref):
    @pl.when(chosen)
    def _():
        lower(this_ref, low_ref)

    @pl.when(jnp.logical_not(chosen))
    def _():
        lower(that_ref, low_ref)


def terms(logits):
    shrunk = jnp.exp(-jnp.abs(logits))
    total = 1.0 + shrunk
    losses = jnp.maximum(logits, 0.0) + jnp.log(total)
    return losses, jnp.where(logits >= 0.0, 1.0, shrunk) / total


def folded(losses):
    out = losses[:, :LANES]
    for at in range(LANES, losses.shape[1], LANES):
        out = out + losses[:, at : at + LANES]
    return out


def product(left, right, left_dim, right_dim):
    return lax.dot_general(
        left, right, (((left_dim,), (right_dim,)), ((), ())), preferred_element_type=jnp.float32
    )


def partner_grad(numbers_ref, own_ref, partner_ref, loss_from, loss_to, counts):
    temper, bias = numbers_ref[0], numbers_ref[1]
    loss, grad = 0.0, 0.0
    for at in range(0, partner_ref.shape[0], COLUMNS):
        partner = partner_ref[pl.ds(at, COLUMNS), :]
        losses, chances = terms(temper * product(own_ref[...], partner, 1, 1) + bias)
        loss = loss + folded(losses)
        grad = grad + product((chances * temper).astype(jnp.bfloat16), partner, 1, 0)
    loss_to[...] = loss_from[...] + counts * loss
    return grad


def pair(numbers_ref, own_ref, partner_ref, acc_from, acc_to, loss_from, loss_to, counts):
    acc_to[...] = acc_from[...] + partner_grad(
        numbers_ref, own_ref, partner_ref, loss_from, loss_to, counts
    )


def first_kernel(
    role_ref, numbers_ref, main, other, swapped,
    lows, units, scales, accs, loss_ref, weights_ref, low_ref,
):
    temper, bias = numbers_ref[0], numbers_ref[1]
    core = role_ref[0]
    count = main.shape[0]
    for side, raw in enumerate((main, other)):
        unit, scale = unit_of(raw, slice(None))
        units[side] = unit
        scales[side] = scale
        lows[side] = unit.astype(jnp.bfloat16)
    image_low, text_low = lows.at[core], lows.at[1 - core]
    logits = temper * product(image_low[...], text_low[...], 1, 1) + bias
    row = lax.broadcasted_iota(jnp.int32, (count, count), 0)
    column = lax.broadcasted_iota(jnp.int32, (count, count), 1)
    same = row == column
    losses, chances = terms(jnp.where(same, -logits, logits))
    loss_ref[...] = folded(losses)
    weights = (jnp.where(same, -chances, chances) * temper).astype(jnp.bfloat16)
    weights_ref[...] = weights
    accs[core] = product(weights, text_low[...], 1, 0)
    accs[1 - core] = product(weights_ref[...], image_low[...], 0, 0)
    lower(swapped, low_ref)
    pair(
        numbers_ref, lows.at[1], low_ref, accs.at[1], accs.at[1], loss_ref, loss_ref, core.astype(jnp.float32)
    )


def late_block_kernel(role_ref, lows, second, late_low):
    outer = role_ref[0] == role_ref[1]

    @pl.when(outer)
    def _():
        lower(second, late_low)

    @pl.when(jnp.logical_not(outer))
    def _():
        late_low[...] = lows[0]


def near_block_kernel(role_ref, near_main, of_other, near_low):
    lower_one_of(role_ref[0] == role_ref[1], near_main, of_other, near_low)


def middle_kernel(
    role_ref, numbers_ref, lows, second, near_low, swapped, accs_in, loss_in, accs, loss_ref, low_ref
):
    on_other = role_ref[0].astype(jnp.float32)
    on_main = 1.0 - on_other
    pair(numbers_ref, lows.at[0], near_low, accs_in.at[0], accs.at[0], loss_in, loss_ref, on_main)
    lower(second, low_ref)
    pair(numbers_ref, lows.at[0], low_ref, accs.at[0], accs.at[0], loss_ref, loss_ref, on_main)
    pair(numbers_ref, lows.at[1], swapped, accs_in.at[1], accs.at[1], loss_ref, loss_ref, on_other)


def close_side(
    side, core, numbers_ref, lows, units, scales, accs, partner_ref, loss_from, loss_to,
    image_out, text_out, done_ref, sems,
):
    counts = (side == core).astype(jnp.float32)
    own_low = lows.at[side]

    parts = done_ref.shape[0] // STRIP

    def copy(k, out):
        rows = pl.ds(k * STRIP, STRIP)
        return pltpu.make_async_copy(done_ref.at[rows, :], out.at[rows, :], sems.at[k])

    done_ref[...] = accs[side] + partner_grad(numbers_ref, own_low, partner_ref, loss_from, loss_to, counts)
    for k in range(parts):
        rows = pl.ds(k * STRIP, STRIP)
        grad = done_ref[rows, :]
        unit = units[side, rows, :]
        along = jnp.sum(unit * grad, axis=-1, keepdims=True)
        done_ref[rows, :] = scales[side, rows, :] * (grad - unit * along)

        @pl.when(side == core)
        def _():
            copy(k, image_out).start()

        @pl.when(side != core)
        def _():
            copy(k, text_out).start()

    @pl.when(side == core)
    def _():
        for k in range(parts):
            copy(k, image_out).wait()

    @pl.when(side != core)
    def _():
        for k in range(parts):
            copy(k, text_out).wait()


def early_kernel(
    role_ref, numbers_ref, lows, units, scales, accs, of_other, by_two, loss_in,
    image_out, text_out, loss_ref, low_ref, done_ref, sems,
):
    outer = role_ref[0] == role_ref[1]
    lower_one_of(outer, of_other, by_two, low_ref)
    close_side(
        jnp.where(outer, 0, 1), role_ref[0], numbers_ref, lows, units, scales, accs, low_ref,
        loss_in, loss_ref, image_out, text_out, done_ref, sems,
    )


def late_kernel(
    role_ref, numbers_ref, lows, units, scales, accs, late_low, loss_in, image_in, text_in,
    image_out, text_out, row_loss, loss_ref, done_ref, sems,
):
    outer = role_ref[0] == role_ref[1]
    close_side(
        jnp.where(outer, 1, 0), role_ref[0], numbers_ref, lows, units, scales, accs, late_low,
        loss_in, loss_ref, image_out, text_out, done_ref, sems,
    )
    row_loss[...] = jnp.sum(loss_ref[...].T, axis=0, keepdims=True)


def call(kernel, in_kinds, outs, scratch=(), aliases=None):
    kinds = {
        "s": pl.BlockSpec(memory_space=pltpu.SMEM),
        "v": pl.BlockSpec(memory_space=pltpu.VMEM),
        "a": pl.BlockSpec(memory_space=pl.ANY),
    }
    return pl.pallas_call(
        kernel,
        in_specs=[kinds[k] for k in in_kinds],
        out_specs=[kinds[k] for k, _, _ in outs],
        out_shape=[jax.ShapeDtypeStruct(shape, dtype) for _, shape, dtype in outs],
        scratch_shapes=list(scratch),
        input_output_aliases=aliases or {},
        compiler_params=pltpu.CompilerParams(vmem_limit_bytes=24 * 1024 * 1024),
    )


def body(image_emb, text_emb, log_temp, bias):
    rows, width = image_emb.shape
    place = lax.axis_index(AXES)
    core = (place // 2) % 2
    role = jnp.stack([core, place % 2]).astype(jnp.int32)
    numbers = jnp.stack([jnp.exp(log_temp), bias])
    is_core_1 = core == 1
    other, image_late, text_late = together(jnp.where(is_core_1, image_emb, text_emb), image_emb, text_emb)
    main = jnp.where(is_core_1, text_late, image_late)

    swapped = send(other, SWAP)
    of_other = send(other, OF_OTHER)
    second = send(main, SECOND)
    near_main = send(main, NEAR_OF_MAIN)

    f32, low = jnp.float32, jnp.bfloat16
    whole, partial, both = (rows, width), (rows, LANES), (2, rows, width)
    lows, units, scales, accs, loss = call(
        first_kernel,
        "ssvvv",
        [("v", both, low), ("v", both, f32), ("v", (2, rows, 1), f32), ("v", both, f32), ("v", partial, f32)],
        [pltpu.VMEM((rows, rows), low), pltpu.VMEM(whole, low)],
    )(role, numbers, main, other, swapped)

    second, near_main, loss = together(second, near_main, loss)
    (late_low,) = call(late_block_kernel, "svv", [("v", whole, low)])(role, lows, second)
    of_other, late_low = together(of_other, late_low)
    by_two = send(of_other, ON_BY_TWO)
    late_low = send(late_low, FAR_OR_ON_BY_ONE)
    (near_low,) = call(near_block_kernel, "svv", [("v", whole, low)])(role, near_main, of_other)
    swapped = send(near_low, SWAP)

    accs, loss = call(
        middle_kernel,
        "ssvvvvvv",
        [("v", both, f32), ("v", partial, f32)],
        [pltpu.VMEM(whole, low)],
        {6: 0, 7: 1},
    )(role, numbers, lows, second, near_low, swapped, accs, loss)

    copy_sems = pltpu.SemaphoreType.DMA((rows // STRIP,))
    grad_image, grad_text, loss = call(
        early_kernel,
        "ssvvvvvvv",
        [("a", whole, f32), ("a", whole, f32), ("v", partial, f32)],
        [pltpu.VMEM(whole, low), pltpu.VMEM(whole, f32), copy_sems],
        {8: 2},
    )(role, numbers, lows, units, scales, accs, of_other, by_two, loss)
    grad_image, grad_text, row_loss = call(
        late_kernel,
        "ssvvvvvvaa",
        [("a", whole, f32), ("a", whole, f32), ("v", (1, rows), f32)],
        [pltpu.VMEM(partial, f32), pltpu.VMEM(whole, f32), copy_sems],
        {8: 0, 9: 1},
    )(role, numbers, lows, units, scales, accs, late_low, loss, grad_image, grad_text)
    return (row_loss.reshape(rows), grad_image, grad_text)


def solution(mesh):
    return jax.shard_map(
        body,
        mesh=mesh,
        in_specs=(P(AXES, None), P(AXES, None), P(), P()),
        out_specs=(P(AXES), P(AXES, None), P(AXES, None)),
        check_vma=False,
    )
```

```python
import functools

import jax
import jax.numpy as jnp
from jax import lax
from jax.experimental import pallas as pl
from jax.experimental.pallas import tpu as pltpu
from jax.sharding import PartitionSpec as P

AXES = ("blk", "rep")
EPSILON = 1e-06
COLUMNS = 512
STRIP = 128
LANES = 128


def by_role(steps):
    def pairs():
        count = lax.axis_size(AXES)
        return [(b, (b + steps[b % 8]) % count) for b in range(count) if b % 8 in steps]

    return pairs


SWAP = by_role({0: 2, 1: 2, 4: 2, 5: 2, 2: -2, 3: -2, 6: -2, 7: -2})
SECOND = by_role({0: -2, 1: -2, 4: -2, 5: -2, 2: 2, 3: 2, 6: 2, 7: 2})
OF_OTHER = by_role({1: 3, 5: 3, 2: -3, 6: -3, 0: 1, 4: 1, 3: -1, 7: -1})
NEAR_OF_MAIN = by_role({0: -1, 4: -1, 3: 1, 7: 1})
NEAR_TO_INNER = by_role({0: 2, 4: 2, 3: -2, 7: -2})
NEAR_TO_OUTER = by_role({1: 2, 5: 2, 2: -2, 6: -2})
ON_BY_TWO = by_role({0: -2, 4: -2, 3: 2, 7: 2})
FAR_OR_ON_BY_ONE = by_role({1: -3, 5: -3, 2: 3, 6: 3, 0: -1, 4: -1, 3: 1, 7: 1})


def send(x, pairs):
    return lax.ppermute(x, AXES, pairs())


def together(*arrays):
    return lax.optimization_barrier(arrays)


def unit_of(raw_ref, rows):
    values = raw_ref[rows, :].astype(jnp.float32)
    scale = lax.rsqrt(jnp.sum(values * values, axis=-1, keepdims=True) + EPSILON)
    return values * scale, scale


def lower(raw_ref, low_ref):
    low_ref[...] = unit_of(raw_ref, slice(None))[0].astype(jnp.bfloat16)


def lower_one_of(chosen, this_ref, that_ref, low_ref):
    @pl.when(chosen)
    def _():
        lower(this_ref, low_ref)

    @pl.when(jnp.logical_not(chosen))
    def _():
        lower(that_ref, low_ref)


def terms(logits):
    shrunk = jnp.exp(-jnp.abs(logits))
    total = 1.0 + shrunk
    losses = jnp.maximum(logits, 0.0) + jnp.log(total)
    return losses, jnp.where(logits >= 0.0, 1.0, shrunk) / total


def folded(losses):
    out = losses[:, :LANES]
    for at in range(LANES, losses.shape[1], LANES):
        out = out + losses[:, at : at + LANES]
    return out


def product(left, right, left_dim, right_dim):
    return lax.dot_general(
        left, right, (((left_dim,), (right_dim,)), ((), ())), preferred_element_type=jnp.float32
    )


def partner_grad(numbers_ref, own_ref, partner_ref, loss_from, loss_to, counts):
    temper, bias = numbers_ref[0], numbers_ref[1]
    loss, grad = 0.0, 0.0
    for at in range(0, partner_ref.shape[0], COLUMNS):
        partner = partner_ref[pl.ds(at, COLUMNS), :]
        losses, chances = terms(temper * product(own_ref[...], partner, 1, 1) + bias)
        loss = loss + folded(losses)
        grad = grad + product((chances * temper).astype(jnp.bfloat16), partner, 1, 0)
    loss_to[...] = loss_from[...] + counts * loss
    return grad


def pair(numbers_ref, own_ref, partner_ref, acc_from, acc_to, loss_from, loss_to, counts):
    acc_to[...] = acc_from[...] + partner_grad(
        numbers_ref, own_ref, partner_ref, loss_from, loss_to, counts
    )


def first_kernel(
    role_ref, numbers_ref, main, other, swapped,
    lows, units, scales, accs, loss_ref, weights_ref, low_ref,
):
    temper, bias = numbers_ref[0], numbers_ref[1]
    core = role_ref[0]
    count = main.shape[0]
    for side, raw in enumerate((main, other)):
        unit, scale = unit_of(raw, slice(None))
        units[side] = unit
        scales[side] = scale
        lows[side] = unit.astype(jnp.bfloat16)
    image_low, text_low = lows.at[core], lows.at[1 - core]
    logits = temper * product(image_low[...], text_low[...], 1, 1) + bias
    row = lax.broadcasted_iota(jnp.int32, (count, count), 0)
    column = lax.broadcasted_iota(jnp.int32, (count, count), 1)
    same = row == column
    losses, chances = terms(jnp.where(same, -logits, logits))
    loss_ref[...] = folded(losses)
    weights = (jnp.where(same, -chances, chances) * temper).astype(jnp.bfloat16)
    weights_ref[...] = weights
    accs[core] = product(weights, text_low[...], 1, 0)
    accs[1 - core] = product(weights_ref[...], image_low[...], 0, 0)
    lower(swapped, low_ref)
    pair(
        numbers_ref, lows.at[1], low_ref, accs.at[1], accs.at[1], loss_ref, loss_ref, core.astype(jnp.float32)
    )


def late_block_kernel(role_ref, lows, second, late_low):
    outer = role_ref[0] == role_ref[1]

    @pl.when(outer)
    def _():
        lower(second, late_low)

    @pl.when(jnp.logical_not(outer))
    def _():
        late_low[...] = lows[0]


def middle_kernel(
    role_ref, numbers_ref, lows, second, near_main, of_other, to_inner, to_outer, accs_in, loss_in,
    accs, loss_ref, low_ref,
):
    on_other = role_ref[0].astype(jnp.float32)
    on_main = 1.0 - on_other
    outer = role_ref[0] == role_ref[1]
    lower(second, low_ref)
    pair(numbers_ref, lows.at[0], low_ref, accs_in.at[0], accs.at[0], loss_in, loss_ref, on_main)
    lower_one_of(outer, near_main, of_other, low_ref)
    pair(numbers_ref, lows.at[0], low_ref, accs.at[0], accs.at[0], loss_ref, loss_ref, on_main)
    lower_one_of(outer, to_outer, to_inner, low_ref)
    pair(numbers_ref, lows.at[1], low_ref, accs_in.at[1], accs.at[1], loss_ref, loss_ref, on_other)


def close_side(
    strip, side, core, numbers_ref, lows, units, scales, accs, partner_ref, loss_from, loss_to,
    image_out, text_out, done_ref, sems,
):
    counts = (side == core).astype(jnp.float32)
    done_ref[...] = accs[side] + partner_grad(
        numbers_ref, lows.at[side], partner_ref, loss_from, loss_to, counts
    )

    def finish_into(out):
        copies = []
        for k in range(done_ref.shape[0] // strip):
            rows = pl.ds(k * strip, strip)
            grad = done_ref[rows, :]
            unit = units[side, rows, :]
            along = jnp.sum(unit * grad, axis=-1, keepdims=True)
            done_ref[rows, :] = scales[side, rows, :] * (grad - unit * along)
            copies.append(pltpu.make_async_copy(done_ref.at[rows, :], out.at[rows, :], sems.at[k]))
            copies[-1].start()
        for copy in copies:
            copy.wait()

    @pl.when(side == core)
    def _():
        finish_into(image_out)

    @pl.when(side != core)
    def _():
        finish_into(text_out)


def early_kernel(
    role_ref, numbers_ref, lows, units, scales, accs, of_other, by_two, loss_in,
    image_out, text_out, loss_ref, low_ref, done_ref, sems,
):
    outer = role_ref[0] == role_ref[1]
    lower_one_of(outer, of_other, by_two, low_ref)
    close_side(
        STRIP, jnp.where(outer, 0, 1), role_ref[0], numbers_ref, lows, units, scales, accs, low_ref,
        loss_in, loss_ref, image_out, text_out, done_ref, sems,
    )


def late_kernel(
    role_ref, numbers_ref, lows, units, scales, accs, late_low, loss_in, image_in, text_in,
    image_out, text_out, row_loss, loss_ref, done_ref, sems,
):
    outer = role_ref[0] == role_ref[1]
    close_side(
        STRIP, jnp.where(outer, 1, 0), role_ref[0], numbers_ref, lows, units, scales, accs, late_low,
        loss_in, loss_ref, image_out, text_out, done_ref, sems,
    )
    row_loss[...] = jnp.sum(loss_ref[...].T, axis=0, keepdims=True)


def call(kernel, in_kinds, outs, scratch=(), aliases=None):
    kinds = {
        "s": pl.BlockSpec(memory_space=pltpu.SMEM),
        "v": pl.BlockSpec(memory_space=pltpu.VMEM),
        "a": pl.BlockSpec(memory_space=pl.ANY),
    }
    return pl.pallas_call(
        kernel,
        in_specs=[kinds[k] for k in in_kinds],
        out_specs=[kinds[k] for k, _, _ in outs],
        out_shape=[jax.ShapeDtypeStruct(shape, dtype) for _, shape, dtype in outs],
        scratch_shapes=list(scratch),
        input_output_aliases=aliases or {},
        compiler_params=pltpu.CompilerParams(vmem_limit_bytes=24 * 1024 * 1024),
    )


def body(image_emb, text_emb, log_temp, bias):
    rows, width = image_emb.shape
    place = lax.axis_index(AXES)
    core = (place // 2) % 2
    role = jnp.stack([core, place % 2]).astype(jnp.int32)
    numbers = jnp.stack([jnp.exp(log_temp), bias])
    is_core_1 = core == 1
    other, image_late, text_late = together(jnp.where(is_core_1, image_emb, text_emb), image_emb, text_emb)
    main = jnp.where(is_core_1, text_late, image_late)

    swapped = send(other, SWAP)
    of_other = send(other, OF_OTHER)
    second = send(main, SECOND)
    near_main = send(main, NEAR_OF_MAIN)

    f32, low = jnp.float32, jnp.bfloat16
    whole, partial, both = (rows, width), (rows, LANES), (2, rows, width)
    lows, units, scales, accs, loss = call(
        first_kernel,
        "ssvvv",
        [("v", both, low), ("v", both, f32), ("v", (2, rows, 1), f32), ("v", both, f32), ("v", partial, f32)],
        [pltpu.VMEM((rows, rows), low), pltpu.VMEM(whole, low)],
    )(role, numbers, main, other, swapped)

    near_main, second, loss = together(near_main, second, loss)
    (late_low,) = call(late_block_kernel, "svv", [("v", whole, low)])(role, lows, second)
    of_other, late_low = together(of_other, late_low)
    by_two = send(of_other, ON_BY_TWO)
    late_low = send(late_low, FAR_OR_ON_BY_ONE)
    to_inner = send(near_main, NEAR_TO_INNER)
    to_outer = send(of_other, NEAR_TO_OUTER)

    accs, loss = call(
        middle_kernel,
        "ssvvvvvvvv",
        [("v", both, f32), ("v", partial, f32)],
        [pltpu.VMEM(whole, low)],
        {8: 0, 9: 1},
    )(role, numbers, lows, second, near_main, of_other, to_inner, to_outer, accs, loss)

    copy_sems = pltpu.SemaphoreType.DMA((rows // STRIP,))
    grad_image, grad_text, loss = call(
        early_kernel,
        "ssvvvvvvv",
        [("a", whole, f32), ("a", whole, f32), ("v", partial, f32)],
        [pltpu.VMEM(whole, low), pltpu.VMEM(whole, f32), copy_sems],
        {8: 2},
    )(role, numbers, lows, units, scales, accs, of_other, by_two, loss)
    grad_image, grad_text, row_loss = call(
        late_kernel,
        "ssvvvvvvaa",
        [("a", whole, f32), ("a", whole, f32), ("v", (1, rows), f32)],
        [pltpu.VMEM(partial, f32), pltpu.VMEM(whole, f32), copy_sems],
        {8: 0, 9: 1},
    )(role, numbers, lows, units, scales, accs, late_low, loss, grad_image, grad_text)
    return (row_loss.reshape(rows), grad_image, grad_text)


def solution(mesh):
    return jax.shard_map(
        body,
        mesh=mesh,
        in_specs=(P(AXES, None), P(AXES, None), P(), P()),
        out_specs=(P(AXES), P(AXES, None), P(AXES, None)),
        check_vma=False,
    )
```

```python
import functools

import jax
import jax.numpy as jnp
from jax import lax
from jax.experimental import pallas as pl
from jax.experimental.pallas import tpu as pltpu
from jax.sharding import PartitionSpec as P

AXES = ("blk", "rep")
EPSILON = 1e-06
STRIP = 256
LANES = 128


def by_role(steps):
    def pairs():
        count = lax.axis_size(AXES)
        return [(b, (b + steps[b % 8]) % count) for b in range(count) if b % 8 in steps]

    return pairs


SWAP = by_role({0: 2, 1: 2, 4: 2, 5: 2, 2: -2, 3: -2, 6: -2, 7: -2})
SECOND = by_role({0: -2, 1: -2, 4: -2, 5: -2, 2: 2, 3: 2, 6: 2, 7: 2})
OF_OTHER = by_role({1: 3, 5: 3, 2: -3, 6: -3, 0: 1, 4: 1, 3: -1, 7: -1})
NEAR_OF_MAIN = by_role({0: -1, 4: -1, 3: 1, 7: 1})
ON_BY_TWO = by_role({0: -2, 4: -2, 3: 2, 7: 2})
FAR_OR_ON_BY_ONE = by_role({1: -3, 5: -3, 2: 3, 6: 3, 0: -1, 4: -1, 3: 1, 7: 1})


def send(x, pairs):
    return lax.ppermute(x, AXES, pairs())


def together(*arrays):
    return lax.optimization_barrier(arrays)


def unit_of(raw_ref, rows):
    values = raw_ref[rows, :].astype(jnp.float32)
    scale = lax.rsqrt(jnp.sum(values * values, axis=-1, keepdims=True) + EPSILON)
    return values * scale, scale


def lower(raw_ref, low_ref):
    low_ref[...] = unit_of(raw_ref, slice(None))[0].astype(jnp.bfloat16)


def lower_one_of(chosen, this_ref, that_ref, low_ref):
    @pl.when(chosen)
    def _():
        lower(this_ref, low_ref)

    @pl.when(jnp.logical_not(chosen))
    def _():
        lower(that_ref, low_ref)


def terms(logits):
    shrunk = jnp.exp(-jnp.abs(logits))
    total = 1.0 + shrunk
    losses = jnp.maximum(logits, 0.0) + jnp.log(total)
    return losses, jnp.where(logits >= 0.0, 1.0, shrunk) / total


def folded(losses):
    out = losses[:, :LANES]
    for at in range(LANES, losses.shape[1], LANES):
        out = out + losses[:, at : at + LANES]
    return out


def product(left, right, left_dim, right_dim):
    return lax.dot_general(
        left, right, (((left_dim,), (right_dim,)), ((), ())), preferred_element_type=jnp.float32
    )


def partner_weights(numbers_ref, own_ref, partner_ref, loss_from, loss_to, counts):
    temper, bias = numbers_ref[0], numbers_ref[1]
    losses, chances = terms(temper * product(own_ref[...], partner_ref[...], 1, 1) + bias)
    loss_to[...] = loss_from[...] + counts * folded(losses)
    return (chances * temper).astype(jnp.bfloat16)


def pair(numbers_ref, own_ref, partner_ref, acc_from, acc_to, loss_from, loss_to, counts):
    weights = partner_weights(numbers_ref, own_ref, partner_ref, loss_from, loss_to, counts)
    acc_to[...] = acc_from[...] + product(weights, partner_ref[...], 1, 0)


def first_kernel(
    role_ref, numbers_ref, main, other, swapped,
    lows, units, scales, accs, loss_ref, weights_ref, low_ref,
):
    temper, bias = numbers_ref[0], numbers_ref[1]
    core = role_ref[0]
    count = main.shape[0]
    for side, raw in enumerate((main, other)):
        unit, scale = unit_of(raw, slice(None))
        units[side] = unit
        scales[side] = scale
        lows[side] = unit.astype(jnp.bfloat16)
    image_low, text_low = lows.at[core], lows.at[1 - core]
    logits = temper * product(image_low[...], text_low[...], 1, 1) + bias
    row = lax.broadcasted_iota(jnp.int32, (count, count), 0)
    column = lax.broadcasted_iota(jnp.int32, (count, count), 1)
    same = row == column
    losses, chances = terms(jnp.where(same, -logits, logits))
    loss_ref[...] = folded(losses)
    weights = (jnp.where(same, -chances, chances) * temper).astype(jnp.bfloat16)
    weights_ref[...] = weights
    accs[core] = product(weights, text_low[...], 1, 0)
    accs[1 - core] = product(weights_ref[...], image_low[...], 0, 0)
    lower(swapped, low_ref)
    pair(
        numbers_ref, lows.at[1], low_ref, accs.at[1], accs.at[1], loss_ref, loss_ref, core.astype(jnp.float32)
    )


def late_block_kernel(role_ref, lows, second, late_low):
    outer = role_ref[0] == role_ref[1]

    @pl.when(outer)
    def _():
        lower(second, late_low)

    @pl.when(jnp.logical_not(outer))
    def _():
        late_low[...] = lows[0]


def middle_kernel(
    role_ref, numbers_ref, lows, near_main, second, of_other, swapped, accs_in, loss_in, accs, loss_ref, low_ref
):
    on_other = role_ref[0].astype(jnp.float32)
    on_main = 1.0 - on_other
    lower_one_of(role_ref[0] == role_ref[1], near_main, of_other, low_ref)
    pair(numbers_ref, lows.at[0], low_ref, accs_in.at[0], accs.at[0], loss_in, loss_ref, on_main)
    lower(second, low_ref)
    pair(numbers_ref, lows.at[0], low_ref, accs.at[0], accs.at[0], loss_ref, loss_ref, on_main)
    lower(swapped, low_ref)
    pair(numbers_ref, lows.at[1], low_ref, accs_in.at[1], accs.at[1], loss_ref, loss_ref, on_other)


def close_side(
    side, core, numbers_ref, lows, units, scales, accs, partner_ref, loss_from, loss_to,
    image_out, text_out, weights_ref, done_ref, sems,
):
    counts = (side == core).astype(jnp.float32)
    weights_ref[...] = partner_weights(numbers_ref, lows.at[side], partner_ref, loss_from, loss_to, counts)

    def finish_into(out):
        copies = []
        for k in range(done_ref.shape[0] // STRIP):
            rows = pl.ds(k * STRIP, STRIP)
            grad = accs[side, rows, :] + product(weights_ref[rows, :], partner_ref[...], 1, 0)
            unit = units[side, rows, :]
            along = jnp.sum(unit * grad, axis=-1, keepdims=True)
            done_ref[rows, :] = scales[side, rows, :] * (grad - unit * along)
            copies.append(pltpu.make_async_copy(done_ref.at[rows, :], out.at[rows, :], sems.at[k]))
            copies[-1].start()
        for copy in copies:
            copy.wait()

    @pl.when(side == core)
    def _():
        finish_into(image_out)

    @pl.when(side != core)
    def _():
        finish_into(text_out)


def early_kernel(
    role_ref, numbers_ref, lows, units, scales, accs, of_other, by_two, loss_in,
    image_out, text_out, loss_ref, low_ref, weights_ref, done_ref, sems,
):
    outer = role_ref[0] == role_ref[1]
    lower_one_of(outer, of_other, by_two, low_ref)
    close_side(
        jnp.where(outer, 0, 1), role_ref[0], numbers_ref, lows, units, scales, accs, low_ref,
        loss_in, loss_ref, image_out, text_out, weights_ref, done_ref, sems,
    )


def late_kernel(
    role_ref, numbers_ref, lows, units, scales, accs, late_low, loss_in, image_in, text_in,
    image_out, text_out, row_loss, loss_ref, weights_ref, done_ref, sems,
):
    outer = role_ref[0] == role_ref[1]
    close_side(
        jnp.where(outer, 1, 0), role_ref[0], numbers_ref, lows, units, scales, accs, late_low,
        loss_in, loss_ref, image_out, text_out, weights_ref, done_ref, sems,
    )
    row_loss[...] = jnp.sum(loss_ref[...].T, axis=0, keepdims=True)


def call(kernel, in_kinds, outs, scratch=(), aliases=None):
    kinds = {
        "s": pl.BlockSpec(memory_space=pltpu.SMEM),
        "v": pl.BlockSpec(memory_space=pltpu.VMEM),
        "a": pl.BlockSpec(memory_space=pl.ANY),
    }
    return pl.pallas_call(
        kernel,
        in_specs=[kinds[k] for k in in_kinds],
        out_specs=[kinds[k] for k, _, _ in outs],
        out_shape=[jax.ShapeDtypeStruct(shape, dtype) for _, shape, dtype in outs],
        scratch_shapes=list(scratch),
        input_output_aliases=aliases or {},
        compiler_params=pltpu.CompilerParams(vmem_limit_bytes=24 * 1024 * 1024),
    )


def body(image_emb, text_emb, log_temp, bias):
    rows, width = image_emb.shape
    place = lax.axis_index(AXES)
    core = (place // 2) % 2
    role = jnp.stack([core, place % 2]).astype(jnp.int32)
    numbers = jnp.stack([jnp.exp(log_temp), bias])
    is_core_1 = core == 1
    other, image_late, text_late = together(jnp.where(is_core_1, image_emb, text_emb), image_emb, text_emb)
    main = jnp.where(is_core_1, text_late, image_late)

    swapped = send(other, SWAP)
    of_other = send(other, OF_OTHER)
    second = send(main, SECOND)
    near_main = send(main, NEAR_OF_MAIN)

    f32, low = jnp.float32, jnp.bfloat16
    whole, partial, both = (rows, width), (rows, LANES), (2, rows, width)
    lows, units, scales, accs, loss = call(
        first_kernel,
        "ssvvv",
        [("v", both, low), ("v", both, f32), ("v", (2, rows, 1), f32), ("v", both, f32), ("v", partial, f32)],
        [pltpu.VMEM((rows, rows), low), pltpu.VMEM(whole, low)],
    )(role, numbers, main, other, swapped)

    second, near_main, loss = together(second, near_main, loss)
    (late_low,) = call(late_block_kernel, "svv", [("v", whole, low)])(role, lows, second)
    of_other, late_low = together(of_other, late_low)
    by_two = send(of_other, ON_BY_TWO)
    late_low = send(late_low, FAR_OR_ON_BY_ONE)
    swapped = send(jnp.where(core == place % 2, near_main, of_other), SWAP)

    accs, loss = call(
        middle_kernel,
        "ssvvvvvvv",
        [("v", both, f32), ("v", partial, f32)],
        [pltpu.VMEM(whole, low)],
        {7: 0, 8: 1},
    )(role, numbers, lows, near_main, second, of_other, swapped, accs, loss)

    copy_sems = pltpu.SemaphoreType.DMA((rows // STRIP,))
    grad_image, grad_text, loss = call(
        early_kernel,
        "ssvvvvvvv",
        [("a", whole, f32), ("a", whole, f32), ("v", partial, f32)],
        [pltpu.VMEM(whole, low), pltpu.VMEM((rows, rows), low), pltpu.VMEM(whole, f32), copy_sems],
        {8: 2},
    )(role, numbers, lows, units, scales, accs, of_other, by_two, loss)
    grad_image, grad_text, row_loss = call(
        late_kernel,
        "ssvvvvvvaa",
        [("a", whole, f32), ("a", whole, f32), ("v", (1, rows), f32)],
        [pltpu.VMEM(partial, f32), pltpu.VMEM((rows, rows), low), pltpu.VMEM(whole, f32), copy_sems],
        {8: 0, 9: 1},
    )(role, numbers, lows, units, scales, accs, late_low, loss, grad_image, grad_text)
    return (row_loss.reshape(rows), grad_image, grad_text)


def solution(mesh):
    return jax.shard_map(
        body,
        mesh=mesh,
        in_specs=(P(AXES, None), P(AXES, None), P(), P()),
        out_specs=(P(AXES), P(AXES, None), P(AXES, None)),
        check_vma=False,
    )
```

```python
import functools

import jax
import jax.numpy as jnp
from jax import lax
from jax.experimental import pallas as pl
from jax.experimental.pallas import tpu as pltpu
from jax.sharding import PartitionSpec as P

AXES = ("blk", "rep")
EPSILON = 1e-06
STRIP = 256
LANES = 128


def by_role(steps):
    def pairs():
        count = lax.axis_size(AXES)
        return [(b, (b + steps[b % 8]) % count) for b in range(count) if b % 8 in steps]

    return pairs


SWAP = by_role({0: 2, 1: 2, 4: 2, 5: 2, 2: -2, 3: -2, 6: -2, 7: -2})
SECOND = by_role({0: -2, 1: -2, 4: -2, 5: -2, 2: 2, 3: 2, 6: 2, 7: 2})
OF_OTHER = by_role({1: 3, 5: 3, 2: -3, 6: -3, 0: 1, 4: 1, 3: -1, 7: -1})
NEAR_OF_MAIN = by_role({0: -1, 4: -1, 3: 1, 7: 1})
ON_BY_TWO = by_role({0: -2, 4: -2, 3: 2, 7: 2})
FAR_OR_ON_BY_ONE = by_role({1: -3, 5: -3, 2: 3, 6: 3, 0: -1, 4: -1, 3: 1, 7: 1})


def send(x, pairs):
    return lax.ppermute(x, AXES, pairs())


def together(*arrays):
    return lax.optimization_barrier(arrays)


def unit_of(raw_ref, rows):
    values = raw_ref[rows, :].astype(jnp.float32)
    scale = lax.rsqrt(jnp.sum(values * values, axis=-1, keepdims=True) + EPSILON)
    return values * scale, scale


def lower(raw_ref, low_ref):
    low_ref[...] = unit_of(raw_ref, slice(None))[0].astype(jnp.bfloat16)


def lower_one_of(chosen, this_ref, that_ref, low_ref):
    @pl.when(chosen)
    def _():
        lower(this_ref, low_ref)

    @pl.when(jnp.logical_not(chosen))
    def _():
        lower(that_ref, low_ref)


def terms(logits):
    shrunk = jnp.exp(-jnp.abs(logits))
    total = 1.0 + shrunk
    losses = jnp.maximum(logits, 0.0) + jnp.log(total)
    return losses, jnp.where(logits >= 0.0, 1.0, shrunk) / total


def folded(losses):
    out = losses[:, :LANES]
    for at in range(LANES, losses.shape[1], LANES):
        out = out + losses[:, at : at + LANES]
    return out


def product(left, right, left_dim, right_dim):
    return lax.dot_general(
        left, right, (((left_dim,), (right_dim,)), ((), ())), preferred_element_type=jnp.float32
    )


def partner_weights(numbers_ref, own_ref, partner_ref, loss_from, loss_to, counts):
    temper, bias = numbers_ref[0], numbers_ref[1]
    losses, chances = terms(temper * product(own_ref[...], partner_ref[...], 1, 1) + bias)
    loss_to[...] = loss_from[...] + counts * folded(losses)
    return (chances * temper).astype(jnp.bfloat16)


def pair(numbers_ref, own_ref, partner_ref, acc_from, acc_to, loss_from, loss_to, counts):
    weights = partner_weights(numbers_ref, own_ref, partner_ref, loss_from, loss_to, counts)
    acc_to[...] = acc_from[...] + product(weights, partner_ref[...], 1, 0)


def first_kernel(
    role_ref, numbers_ref, main, other, swapped,
    lows, units, scales, accs, loss_ref, weights_ref, low_ref,
):
    temper, bias = numbers_ref[0], numbers_ref[1]
    core = role_ref[0]
    count = main.shape[0]
    for side, raw in enumerate((main, other)):
        unit, scale = unit_of(raw, slice(None))
        units[side] = unit
        scales[side] = scale
        lows[side] = unit.astype(jnp.bfloat16)
    image_low, text_low = lows.at[core], lows.at[1 - core]
    logits = temper * product(image_low[...], text_low[...], 1, 1) + bias
    row = lax.broadcasted_iota(jnp.int32, (count, count), 0)
    column = lax.broadcasted_iota(jnp.int32, (count, count), 1)
    same = row == column
    losses, chances = terms(jnp.where(same, -logits, logits))
    loss_ref[...] = folded(losses)
    weights = (jnp.where(same, -chances, chances) * temper).astype(jnp.bfloat16)
    weights_ref[...] = weights
    accs[core] = product(weights, text_low[...], 1, 0)
    accs[1 - core] = product(weights_ref[...], image_low[...], 0, 0)
    lower(swapped, low_ref)
    pair(
        numbers_ref, lows.at[1], low_ref, accs.at[1], accs.at[1], loss_ref, loss_ref, core.astype(jnp.float32)
    )


def late_block_kernel(role_ref, lows, second, late_low):
    outer = role_ref[0] == role_ref[1]

    @pl.when(outer)
    def _():
        lower(second, late_low)

    @pl.when(jnp.logical_not(outer))
    def _():
        late_low[...] = lows[0]


def middle_kernel(
    role_ref, numbers_ref, lows, near, second, swapped, accs_in, loss_in, accs, loss_ref, low_ref
):
    on_other = role_ref[0].astype(jnp.float32)
    on_main = 1.0 - on_other
    lower(near, low_ref)
    pair(numbers_ref, lows.at[0], low_ref, accs_in.at[0], accs.at[0], loss_in, loss_ref, on_main)
    lower(second, low_ref)
    pair(numbers_ref, lows.at[0], low_ref, accs.at[0], accs.at[0], loss_ref, loss_ref, on_main)
    lower(swapped, low_ref)
    pair(numbers_ref, lows.at[1], low_ref, accs_in.at[1], accs.at[1], loss_ref, loss_ref, on_other)


def close_side(
    side, core, numbers_ref, lows, units, scales, accs, partner_ref, loss_from, loss_to,
    image_out, text_out, weights_ref, done_ref, sems,
):
    counts = (side == core).astype(jnp.float32)
    weights_ref[...] = partner_weights(numbers_ref, lows.at[side], partner_ref, loss_from, loss_to, counts)

    def finish_into(out):
        copies = []
        for k in range(done_ref.shape[0] // STRIP):
            rows = pl.ds(k * STRIP, STRIP)
            grad = accs[side, rows, :] + product(weights_ref[rows, :], partner_ref[...], 1, 0)
            unit = units[side, rows, :]
            along = jnp.sum(unit * grad, axis=-1, keepdims=True)
            done_ref[rows, :] = scales[side, rows, :] * (grad - unit * along)
            copies.append(pltpu.make_async_copy(done_ref.at[rows, :], out.at[rows, :], sems.at[k]))
            copies[-1].start()
        for copy in copies:
            copy.wait()

    @pl.when(side == core)
    def _():
        finish_into(image_out)

    @pl.when(side != core)
    def _():
        finish_into(text_out)


def early_kernel(
    role_ref, numbers_ref, lows, units, scales, accs, of_other, by_two, loss_in,
    image_out, text_out, loss_ref, low_ref, weights_ref, done_ref, sems,
):
    outer = role_ref[0] == role_ref[1]
    lower_one_of(outer, of_other, by_two, low_ref)
    close_side(
        jnp.where(outer, 0, 1), role_ref[0], numbers_ref, lows, units, scales, accs, low_ref,
        loss_in, loss_ref, image_out, text_out, weights_ref, done_ref, sems,
    )


def late_kernel(
    role_ref, numbers_ref, lows, units, scales, accs, late_low, loss_in, image_in, text_in,
    image_out, text_out, row_loss, loss_ref, weights_ref, done_ref, sems,
):
    outer = role_ref[0] == role_ref[1]
    close_side(
        jnp.where(outer, 1, 0), role_ref[0], numbers_ref, lows, units, scales, accs, late_low,
        loss_in, loss_ref, image_out, text_out, weights_ref, done_ref, sems,
    )
    row_loss[...] = jnp.sum(loss_ref[...].T, axis=0, keepdims=True)


def call(kernel, in_kinds, outs, scratch=(), aliases=None):
    kinds = {
        "s": pl.BlockSpec(memory_space=pltpu.SMEM),
        "v": pl.BlockSpec(memory_space=pltpu.VMEM),
        "a": pl.BlockSpec(memory_space=pl.ANY),
    }
    return pl.pallas_call(
        kernel,
        in_specs=[kinds[k] for k in in_kinds],
        out_specs=[kinds[k] for k, _, _ in outs],
        out_shape=[jax.ShapeDtypeStruct(shape, dtype) for _, shape, dtype in outs],
        scratch_shapes=list(scratch),
        input_output_aliases=aliases or {},
        compiler_params=pltpu.CompilerParams(vmem_limit_bytes=24 * 1024 * 1024),
    )


def body(image_emb, text_emb, log_temp, bias):
    rows, width = image_emb.shape
    place = lax.axis_index(AXES)
    core = (place // 2) % 2
    role = jnp.stack([core, place % 2]).astype(jnp.int32)
    numbers = jnp.stack([jnp.exp(log_temp), bias])
    is_core_1 = core == 1
    main = jnp.where(is_core_1, text_emb, image_emb)
    other = jnp.where(is_core_1, image_emb, text_emb)
    main, other = together(main, other)

    swapped = send(other, SWAP)
    of_other = send(other, OF_OTHER)
    second = send(main, SECOND)
    near_main = send(main, NEAR_OF_MAIN)

    f32, low = jnp.float32, jnp.bfloat16
    whole, partial, both = (rows, width), (rows, LANES), (2, rows, width)
    lows, units, scales, accs, loss = call(
        first_kernel,
        "ssvvv",
        [("v", both, low), ("v", both, f32), ("v", (2, rows, 1), f32), ("v", both, f32), ("v", partial, f32)],
        [pltpu.VMEM((rows, rows), low), pltpu.VMEM(whole, low)],
    )(role, numbers, main, other, swapped)

    second, near_main, loss = together(second, near_main, loss)
    (late_low,) = call(late_block_kernel, "svv", [("v", whole, low)])(role, lows, second)
    of_other, late_low = together(of_other, late_low)
    by_two = send(of_other, ON_BY_TWO)
    late_low = send(late_low, FAR_OR_ON_BY_ONE)
    near = jnp.where(core == place % 2, near_main, of_other)
    swapped = send(near, SWAP)

    accs, loss = call(
        middle_kernel,
        "ssvvvvvv",
        [("v", both, f32), ("v", partial, f32)],
        [pltpu.VMEM(whole, low)],
        {6: 0, 7: 1},
    )(role, numbers, lows, near, second, swapped, accs, loss)

    copy_sems = pltpu.SemaphoreType.DMA((rows // STRIP,))
    grad_image, grad_text, loss = call(
        early_kernel,
        "ssvvvvvvv",
        [("a", whole, f32), ("a", whole, f32), ("v", partial, f32)],
        [pltpu.VMEM(whole, low), pltpu.VMEM((rows, rows), low), pltpu.VMEM(whole, f32), copy_sems],
        {8: 2},
    )(role, numbers, lows, units, scales, accs, of_other, by_two, loss)
    grad_image, grad_text, row_loss = call(
        late_kernel,
        "ssvvvvvvaa",
        [("a", whole, f32), ("a", whole, f32), ("v", (1, rows), f32)],
        [pltpu.VMEM(partial, f32), pltpu.VMEM((rows, rows), low), pltpu.VMEM(whole, f32), copy_sems],
        {8: 0, 9: 1},
    )(role, numbers, lows, units, scales, accs, late_low, loss, grad_image, grad_text)
    return (row_loss.reshape(rows), grad_image, grad_text)


def solution(mesh):
    return jax.shard_map(
        body,
        mesh=mesh,
        in_specs=(P(AXES, None), P(AXES, None), P(), P()),
        out_specs=(P(AXES), P(AXES, None), P(AXES, None)),
        check_vma=False,
    )
```

```python
import functools

import jax
import jax.numpy as jnp
from jax import lax
from jax.experimental import pallas as pl
from jax.experimental.pallas import tpu as pltpu
from jax.sharding import PartitionSpec as P

AXES = ("blk", "rep")
EPSILON = 1e-06
STRIP = 256
LANES = 128


def by_role(steps):
    def pairs():
        count = lax.axis_size(AXES)
        return [(b, (b + steps[b % 8]) % count) for b in range(count) if b % 8 in steps]

    return pairs


SWAP = by_role({0: 2, 1: 2, 4: 2, 5: 2, 2: -2, 3: -2, 6: -2, 7: -2})
SECOND = by_role({0: -2, 1: -2, 4: -2, 5: -2, 2: 2, 3: 2, 6: 2, 7: 2})
OF_OTHER = by_role({1: 3, 5: 3, 2: -3, 6: -3, 0: 1, 4: 1, 3: -1, 7: -1})
NEAR_OF_MAIN = by_role({0: -1, 4: -1, 3: 1, 7: 1})
NEAR_TO_INNER = by_role({0: 2, 4: 2, 3: -2, 7: -2})
ON_OR_TO_OUTER = by_role({0: -2, 4: -2, 3: 2, 7: 2, 1: 2, 5: 2, 2: -2, 6: -2})
FAR_OR_ON_BY_ONE = by_role({1: -3, 5: -3, 2: 3, 6: 3, 0: -1, 4: -1, 3: 1, 7: 1})


def send(x, pairs):
    return lax.ppermute(x, AXES, pairs())


def together(*arrays):
    return lax.optimization_barrier(arrays)


def unit_of(raw_ref, rows):
    values = raw_ref[rows, :].astype(jnp.float32)
    scale = lax.rsqrt(jnp.sum(values * values, axis=-1, keepdims=True) + EPSILON)
    return values * scale, scale


def lower(raw_ref, low_ref):
    low_ref[...] = unit_of(raw_ref, slice(None))[0].astype(jnp.bfloat16)


def lower_one_of(chosen, this_ref, that_ref, low_ref):
    @pl.when(chosen)
    def _():
        lower(this_ref, low_ref)

    @pl.when(jnp.logical_not(chosen))
    def _():
        lower(that_ref, low_ref)


def terms(logits):
    shrunk = jnp.exp(-jnp.abs(logits))
    total = 1.0 + shrunk
    losses = jnp.maximum(logits, 0.0) + jnp.log(total)
    return losses, jnp.where(logits >= 0.0, 1.0, shrunk) / total


def folded(losses):
    out = losses[:, :LANES]
    for at in range(LANES, losses.shape[1], LANES):
        out = out + losses[:, at : at + LANES]
    return out


def product(left, right, left_dim, right_dim):
    return lax.dot_general(
        left, right, (((left_dim,), (right_dim,)), ((), ())), preferred_element_type=jnp.float32
    )


def partner_weights(numbers_ref, own_ref, partner_ref, loss_from, loss_to, counts):
    temper, bias = numbers_ref[0], numbers_ref[1]
    losses, chances = terms(temper * product(own_ref[...], partner_ref[...], 1, 1) + bias)
    loss_to[...] = loss_from[...] + counts * folded(losses)
    return (chances * temper).astype(jnp.bfloat16)


def pair(numbers_ref, own_ref, partner_ref, acc_from, acc_to, loss_from, loss_to, counts):
    weights = partner_weights(numbers_ref, own_ref, partner_ref, loss_from, loss_to, counts)
    acc_to[...] = acc_from[...] + product(weights, partner_ref[...], 1, 0)


def first_kernel(
    role_ref, numbers_ref, main, other, swapped,
    lows, units, scales, accs, loss_ref, weights_ref, low_ref,
):
    temper, bias = numbers_ref[0], numbers_ref[1]
    core = role_ref[0]
    count = main.shape[0]
    for side, raw in enumerate((main, other)):
        unit, scale = unit_of(raw, slice(None))
        units[side] = unit
        scales[side] = scale
        lows[side] = unit.astype(jnp.bfloat16)
    image_low, text_low = lows.at[core], lows.at[1 - core]
    logits = temper * product(image_low[...], text_low[...], 1, 1) + bias
    row = lax.broadcasted_iota(jnp.int32, (count, count), 0)
    column = lax.broadcasted_iota(jnp.int32, (count, count), 1)
    same = row == column
    losses, chances = terms(jnp.where(same, -logits, logits))
    loss_ref[...] = folded(losses)
    weights = (jnp.where(same, -chances, chances) * temper).astype(jnp.bfloat16)
    weights_ref[...] = weights
    accs[core] = product(weights, text_low[...], 1, 0)
    accs[1 - core] = product(weights_ref[...], image_low[...], 0, 0)
    lower(swapped, low_ref)
    pair(
        numbers_ref, lows.at[1], low_ref, accs.at[1], accs.at[1], loss_ref, loss_ref, core.astype(jnp.float32)
    )


def late_block_kernel(role_ref, lows, second, late_low):
    outer = role_ref[0] == role_ref[1]

    @pl.when(outer)
    def _():
        lower(second, late_low)

    @pl.when(jnp.logical_not(outer))
    def _():
        late_low[...] = lows[0]


def middle_kernel(
    role_ref, numbers_ref, lows, near_main, second, of_other, accs_in, loss_in, accs, loss_ref, low_ref
):
    on_main = 1.0 - role_ref[0].astype(jnp.float32)
    lower_one_of(role_ref[0] == role_ref[1], near_main, of_other, low_ref)
    pair(numbers_ref, lows.at[0], low_ref, accs_in.at[0], accs.at[0], loss_in, loss_ref, on_main)
    lower(second, low_ref)
    pair(numbers_ref, lows.at[0], low_ref, accs.at[0], accs.at[0], loss_ref, loss_ref, on_main)
    accs[1] = accs_in[1]


def close_side(
    side, core, numbers_ref, lows, units, scales, accs, partner_ref, loss_from, loss_to,
    image_out, text_out, weights_ref, done_ref, sems,
):
    counts = (side == core).astype(jnp.float32)
    weights_ref[...] = partner_weights(numbers_ref, lows.at[side], partner_ref, loss_from, loss_to, counts)

    def finish_into(out):
        copies = []
        for k in range(done_ref.shape[0] // STRIP):
            rows = pl.ds(k * STRIP, STRIP)
            grad = accs[side, rows, :] + product(weights_ref[rows, :], partner_ref[...], 1, 0)
            unit = units[side, rows, :]
            along = jnp.sum(unit * grad, axis=-1, keepdims=True)
            done_ref[rows, :] = scales[side, rows, :] * (grad - unit * along)
            copies.append(pltpu.make_async_copy(done_ref.at[rows, :], out.at[rows, :], sems.at[k]))
            copies[-1].start()
        for copy in copies:
            copy.wait()

    @pl.when(side == core)
    def _():
        finish_into(image_out)

    @pl.when(side != core)
    def _():
        finish_into(text_out)


def early_kernel(
    role_ref, numbers_ref, lows, units, scales, of_other, by_two, to_inner, accs_in, loss_in,
    image_out, text_out, accs, loss_ref, low_ref, weights_ref, done_ref, sems,
):
    outer = role_ref[0] == role_ref[1]
    lower_one_of(outer, by_two, to_inner, low_ref)
    accs[0] = accs_in[0]
    pair(
        numbers_ref, lows.at[1], low_ref, accs_in.at[1], accs.at[1], loss_in, loss_ref,
        role_ref[0].astype(jnp.float32),
    )
    lower_one_of(outer, of_other, by_two, low_ref)
    close_side(
        jnp.where(outer, 0, 1), role_ref[0], numbers_ref, lows, units, scales, accs, low_ref,
        loss_ref, loss_ref, image_out, text_out, weights_ref, done_ref, sems,
    )


def late_kernel(
    role_ref, numbers_ref, lows, units, scales, accs, late_low, loss_in, image_in, text_in,
    image_out, text_out, row_loss, loss_ref, weights_ref, done_ref, sems,
):
    outer = role_ref[0] == role_ref[1]
    close_side(
        jnp.where(outer, 1, 0), role_ref[0], numbers_ref, lows, units, scales, accs, late_low,
        loss_in, loss_ref, image_out, text_out, weights_ref, done_ref, sems,
    )
    row_loss[...] = jnp.sum(loss_ref[...].T, axis=0, keepdims=True)


def call(kernel, in_kinds, outs, scratch=(), aliases=None):
    kinds = {
        "s": pl.BlockSpec(memory_space=pltpu.SMEM),
        "v": pl.BlockSpec(memory_space=pltpu.VMEM),
        "a": pl.BlockSpec(memory_space=pl.ANY),
    }
    return pl.pallas_call(
        kernel,
        in_specs=[kinds[k] for k in in_kinds],
        out_specs=[kinds[k] for k, _, _ in outs],
        out_shape=[jax.ShapeDtypeStruct(shape, dtype) for _, shape, dtype in outs],
        scratch_shapes=list(scratch),
        input_output_aliases=aliases or {},
        compiler_params=pltpu.CompilerParams(vmem_limit_bytes=24 * 1024 * 1024),
    )


def body(image_emb, text_emb, log_temp, bias):
    rows, width = image_emb.shape
    place = lax.axis_index(AXES)
    core = (place // 2) % 2
    role = jnp.stack([core, place % 2]).astype(jnp.int32)
    numbers = jnp.stack([jnp.exp(log_temp), bias])
    is_core_1 = core == 1
    main = jnp.where(is_core_1, text_emb, image_emb)
    other = jnp.where(is_core_1, image_emb, text_emb)
    main, other = together(main, other)

    swapped = send(other, SWAP)
    of_other = send(other, OF_OTHER)
    second = send(main, SECOND)
    near_main = send(main, NEAR_OF_MAIN)

    f32, low = jnp.float32, jnp.bfloat16
    whole, partial, both = (rows, width), (rows, LANES), (2, rows, width)
    lows, units, scales, accs, loss = call(
        first_kernel,
        "ssvvv",
        [("v", both, low), ("v", both, f32), ("v", (2, rows, 1), f32), ("v", both, f32), ("v", partial, f32)],
        [pltpu.VMEM((rows, rows), low), pltpu.VMEM(whole, low)],
    )(role, numbers, main, other, swapped)

    second, near_main, loss = together(second, near_main, loss)
    (late_low,) = call(late_block_kernel, "svv", [("v", whole, low)])(role, lows, second)
    of_other, late_low = together(of_other, late_low)
    by_two = send(of_other, ON_OR_TO_OUTER)
    late_low = send(late_low, FAR_OR_ON_BY_ONE)
    to_inner = send(near_main, NEAR_TO_INNER)

    accs, loss = call(
        middle_kernel,
        "ssvvvvvv",
        [("v", both, f32), ("v", partial, f32)],
        [pltpu.VMEM(whole, low)],
        {6: 0, 7: 1},
    )(role, numbers, lows, near_main, second, of_other, accs, loss)

    copy_sems = pltpu.SemaphoreType.DMA((rows // STRIP,))
    grad_image, grad_text, accs, loss = call(
        early_kernel,
        "ssvvvvvvvv",
        [("a", whole, f32), ("a", whole, f32), ("v", both, f32), ("v", partial, f32)],
        [pltpu.VMEM(whole, low), pltpu.VMEM((rows, rows), low), pltpu.VMEM(whole, f32), copy_sems],
        {8: 2, 9: 3},
    )(role, numbers, lows, units, scales, of_other, by_two, to_inner, accs, loss)
    grad_image, grad_text, row_loss = call(
        late_kernel,
        "ssvvvvvvaa",
        [("a", whole, f32), ("a", whole, f32), ("v", (1, rows), f32)],
        [pltpu.VMEM(partial, f32), pltpu.VMEM((rows, rows), low), pltpu.VMEM(whole, f32), copy_sems],
        {8: 0, 9: 1},
    )(role, numbers, lows, units, scales, accs, late_low, loss, grad_image, grad_text)
    return (row_loss.reshape(rows), grad_image, grad_text)


def solution(mesh):
    return jax.shard_map(
        body,
        mesh=mesh,
        in_specs=(P(AXES, None), P(AXES, None), P(), P()),
        out_specs=(P(AXES), P(AXES, None), P(AXES, None)),
        check_vma=False,
    )
```

```python
import functools

import jax
import jax.numpy as jnp
from jax import lax
from jax.experimental import pallas as pl
from jax.experimental.pallas import tpu as pltpu
from jax.sharding import PartitionSpec as P

AXES = ("blk", "rep")
EPSILON = 1e-06
STRIP = 256
LANES = 128


def by_role(steps):
    def pairs():
        count = lax.axis_size(AXES)
        return [(b, (b + steps[b % 8]) % count) for b in range(count) if b % 8 in steps]

    return pairs


SWAP = by_role({0: 2, 1: 2, 4: 2, 5: 2, 2: -2, 3: -2, 6: -2, 7: -2})
SECOND = by_role({0: -2, 1: -2, 4: -2, 5: -2, 2: 2, 3: 2, 6: 2, 7: 2})
OF_OTHER = by_role({1: 3, 5: 3, 2: -3, 6: -3, 0: 1, 4: 1, 3: -1, 7: -1})
NEAR_OF_MAIN = by_role({0: -1, 4: -1, 3: 1, 7: 1})
NEAR_TO_INNER = by_role({0: 2, 4: 2, 3: -2, 7: -2})
ON_OR_TO_OUTER = by_role({0: -2, 4: -2, 3: 2, 7: 2, 1: 2, 5: 2, 2: -2, 6: -2})
FAR_OR_ON_BY_ONE = by_role({1: -3, 5: -3, 2: 3, 6: 3, 0: -1, 4: -1, 3: 1, 7: 1})


def send(x, pairs):
    return lax.ppermute(x, AXES, pairs())


def together(*arrays):
    return lax.optimization_barrier(arrays)


def unit_of(raw_ref, rows):
    values = raw_ref[rows, :].astype(jnp.float32)
    scale = lax.rsqrt(jnp.sum(values * values, axis=-1, keepdims=True) + EPSILON)
    return values * scale, scale


def lower(raw_ref, low_ref):
    low_ref[...] = unit_of(raw_ref, slice(None))[0].astype(jnp.bfloat16)


def lower_one_of(chosen, this_ref, that_ref, low_ref):
    @pl.when(chosen)
    def _():
        lower(this_ref, low_ref)

    @pl.when(jnp.logical_not(chosen))
    def _():
        lower(that_ref, low_ref)


def terms(logits):
    shrunk = jnp.exp(-jnp.abs(logits))
    total = 1.0 + shrunk
    losses = jnp.maximum(logits, 0.0) + jnp.log(total)
    return losses, jnp.where(logits >= 0.0, 1.0, shrunk) / total


def folded(losses):
    out = losses[:, :LANES]
    for at in range(LANES, losses.shape[1], LANES):
        out = out + losses[:, at : at + LANES]
    return out


def product(left, right, left_dim, right_dim):
    return lax.dot_general(
        left, right, (((left_dim,), (right_dim,)), ((), ())), preferred_element_type=jnp.float32
    )


def partner_weights(numbers_ref, own_ref, partner_ref, loss_from, loss_to, counts):
    temper, bias = numbers_ref[0], numbers_ref[1]
    losses, chances = terms(temper * product(own_ref[...], partner_ref[...], 1, 1) + bias)
    loss_to[...] = loss_from[...] + counts * folded(losses)
    return (chances * temper).astype(jnp.bfloat16)


def pair(numbers_ref, own_ref, partner_ref, acc_from, acc_to, loss_from, loss_to, counts):
    weights = partner_weights(numbers_ref, own_ref, partner_ref, loss_from, loss_to, counts)
    acc_to[...] = acc_from[...] + product(weights, partner_ref[...], 1, 0)


def first_kernel(
    role_ref, numbers_ref, main, other, swapped,
    lows, units, scales, accs, loss_ref, weights_ref, low_ref,
):
    temper, bias = numbers_ref[0], numbers_ref[1]
    core = role_ref[0]
    count = main.shape[0]
    for side, raw in enumerate((main, other)):
        unit, scale = unit_of(raw, slice(None))
        units[side] = unit
        scales[side] = scale
        lows[side] = unit.astype(jnp.bfloat16)
    image_low, text_low = lows.at[core], lows.at[1 - core]
    logits = temper * product(image_low[...], text_low[...], 1, 1) + bias
    row = lax.broadcasted_iota(jnp.int32, (count, count), 0)
    column = lax.broadcasted_iota(jnp.int32, (count, count), 1)
    same = row == column
    losses, chances = terms(jnp.where(same, -logits, logits))
    loss_ref[...] = folded(losses)
    weights = (jnp.where(same, -chances, chances) * temper).astype(jnp.bfloat16)
    weights_ref[...] = weights
    accs[core] = product(weights, text_low[...], 1, 0)
    accs[1 - core] = product(weights_ref[...], image_low[...], 0, 0)
    lower(swapped, low_ref)
    pair(
        numbers_ref, lows.at[1], low_ref, accs.at[1], accs.at[1], loss_ref, loss_ref, core.astype(jnp.float32)
    )


def late_block_kernel(role_ref, lows, second, late_low):
    outer = role_ref[0] == role_ref[1]

    @pl.when(outer)
    def _():
        lower(second, late_low)

    @pl.when(jnp.logical_not(outer))
    def _():
        late_low[...] = lows[0]


def middle_kernel(
    role_ref, numbers_ref, lows, near_main, second, of_other, accs_in, loss_in, accs, loss_ref, low_ref
):
    on_main = 1.0 - role_ref[0].astype(jnp.float32)
    lower_one_of(role_ref[0] == role_ref[1], near_main, of_other, low_ref)
    pair(numbers_ref, lows.at[0], low_ref, accs_in.at[0], accs.at[0], loss_in, loss_ref, on_main)
    lower(second, low_ref)
    pair(numbers_ref, lows.at[0], low_ref, accs.at[0], accs.at[0], loss_ref, loss_ref, on_main)
    accs[1] = accs_in[1]


def close_side(
    side, core, numbers_ref, lows, units, scales, accs, partner_ref, loss_from, loss_to,
    image_out, text_out, weights_ref, done_ref, sems,
):
    counts = (side == core).astype(jnp.float32)
    weights_ref[...] = partner_weights(numbers_ref, lows.at[side], partner_ref, loss_from, loss_to, counts)

    def finish_into(out):
        copies = []
        for k in range(done_ref.shape[0] // STRIP):
            rows = pl.ds(k * STRIP, STRIP)
            grad = accs[side, rows, :] + product(weights_ref[rows, :], partner_ref[...], 1, 0)
            unit = units[side, rows, :]
            along = jnp.sum(unit * grad, axis=-1, keepdims=True)
            done_ref[rows, :] = scales[side, rows, :] * (grad - unit * along)
            copies.append(pltpu.make_async_copy(done_ref.at[rows, :], out.at[rows, :], sems.at[k]))
            copies[-1].start()
        for copy in copies:
            copy.wait()

    @pl.when(side == core)
    def _():
        finish_into(image_out)

    @pl.when(side != core)
    def _():
        finish_into(text_out)


def early_kernel(
    role_ref, numbers_ref, lows, units, scales, of_other, by_two, to_inner, accs_in, loss_in,
    image_out, text_out, accs, loss_ref, low_ref, weights_ref, done_ref, sems,
):
    outer = role_ref[0] == role_ref[1]
    lower_one_of(outer, by_two, to_inner, low_ref)
    accs[0] = accs_in[0]
    pair(
        numbers_ref, lows.at[1], low_ref, accs_in.at[1], accs.at[1], loss_in, loss_ref,
        role_ref[0].astype(jnp.float32),
    )
    lower_one_of(outer, of_other, by_two, low_ref)
    close_side(
        jnp.where(outer, 0, 1), role_ref[0], numbers_ref, lows, units, scales, accs, low_ref,
        loss_ref, loss_ref, image_out, text_out, weights_ref, done_ref, sems,
    )


def late_kernel(
    role_ref, numbers_ref, lows, units, scales, accs, late_low, loss_in, image_in, text_in,
    image_out, text_out, row_loss, loss_ref, weights_ref, done_ref, sems,
):
    outer = role_ref[0] == role_ref[1]
    close_side(
        jnp.where(outer, 1, 0), role_ref[0], numbers_ref, lows, units, scales, accs, late_low,
        loss_in, loss_ref, image_out, text_out, weights_ref, done_ref, sems,
    )
    row_loss[...] = jnp.sum(loss_ref[...].T, axis=0, keepdims=True)


def call(kernel, in_kinds, outs, scratch=(), aliases=None):
    kinds = {
        "s": pl.BlockSpec(memory_space=pltpu.SMEM),
        "v": pl.BlockSpec(memory_space=pltpu.VMEM),
        "a": pl.BlockSpec(memory_space=pl.ANY),
    }
    return pl.pallas_call(
        kernel,
        in_specs=[kinds[k] for k in in_kinds],
        out_specs=[kinds[k] for k, _, _ in outs],
        out_shape=[jax.ShapeDtypeStruct(shape, dtype) for _, shape, dtype in outs],
        scratch_shapes=list(scratch),
        input_output_aliases=aliases or {},
        compiler_params=pltpu.CompilerParams(vmem_limit_bytes=24 * 1024 * 1024),
    )


def body(image_emb, text_emb, log_temp, bias):
    rows, width = image_emb.shape
    place = lax.axis_index(AXES)
    core = (place // 2) % 2
    role = jnp.stack([core, place % 2]).astype(jnp.int32)
    numbers = jnp.stack([jnp.exp(log_temp), bias])
    is_core_1 = core == 1
    main = jnp.where(is_core_1, text_emb, image_emb)
    other = jnp.where(is_core_1, image_emb, text_emb)
    main, other = together(main, other)

    swapped = send(other, SWAP)
    of_other = send(other, OF_OTHER)
    second = send(main, SECOND)
    near_main = send(main, NEAR_OF_MAIN)

    f32, low = jnp.float32, jnp.bfloat16
    whole, partial, both = (rows, width), (rows, LANES), (2, rows, width)
    lows, units, scales, accs, loss = call(
        first_kernel,
        "ssvvv",
        [("v", both, low), ("v", both, f32), ("v", (2, rows, 1), f32), ("v", both, f32), ("v", partial, f32)],
        [pltpu.VMEM((rows, rows), low), pltpu.VMEM(whole, low)],
    )(role, numbers, main, other, swapped)

    second, near_main, loss = together(second, near_main, loss)
    (late_low,) = call(late_block_kernel, "svv", [("v", whole, low)])(role, lows, second)
    to_inner = send(near_main, NEAR_TO_INNER)
    of_other, late_low, to_inner = together(of_other, late_low, to_inner)
    by_two = send(of_other, ON_OR_TO_OUTER)
    late_low = send(late_low, FAR_OR_ON_BY_ONE)
    accs, loss = call(
        middle_kernel,
        "ssvvvvvv",
        [("v", both, f32), ("v", partial, f32)],
        [pltpu.VMEM(whole, low)],
        {6: 0, 7: 1},
    )(role, numbers, lows, near_main, second, of_other, accs, loss)

    copy_sems = pltpu.SemaphoreType.DMA((rows // STRIP,))
    grad_image, grad_text, accs, loss = call(
        early_kernel,
        "ssvvvvvvvv",
        [("a", whole, f32), ("a", whole, f32), ("v", both, f32), ("v", partial, f32)],
        [pltpu.VMEM(whole, low), pltpu.VMEM((rows, rows), low), pltpu.VMEM(whole, f32), copy_sems],
        {8: 2, 9: 3},
    )(role, numbers, lows, units, scales, of_other, by_two, to_inner, accs, loss)
    grad_image, grad_text, row_loss = call(
        late_kernel,
        "ssvvvvvvaa",
        [("a", whole, f32), ("a", whole, f32), ("v", (1, rows), f32)],
        [pltpu.VMEM(partial, f32), pltpu.VMEM((rows, rows), low), pltpu.VMEM(whole, f32), copy_sems],
        {8: 0, 9: 1},
    )(role, numbers, lows, units, scales, accs, late_low, loss, grad_image, grad_text)
    return (row_loss.reshape(rows), grad_image, grad_text)


def solution(mesh):
    return jax.shard_map(
        body,
        mesh=mesh,
        in_specs=(P(AXES, None), P(AXES, None), P(), P()),
        out_specs=(P(AXES), P(AXES, None), P(AXES, None)),
        check_vma=False,
    )
```

```python
import functools

import jax
import jax.numpy as jnp
from jax import lax
from jax.experimental import pallas as pl
from jax.experimental.pallas import tpu as pltpu
from jax.sharding import PartitionSpec as P

AXES = ("blk", "rep")
EPSILON = 1e-06
STRIP = 256
LANES = 128


def by_role(steps):
    def pairs():
        count = lax.axis_size(AXES)
        return [(b, (b + steps[b % 8]) % count) for b in range(count) if b % 8 in steps]

    return pairs


SWAP = by_role({0: 2, 1: 2, 4: 2, 5: 2, 2: -2, 3: -2, 6: -2, 7: -2})
SECOND = by_role({0: -2, 1: -2, 4: -2, 5: -2, 2: 2, 3: 2, 6: 2, 7: 2})
OF_OTHER = by_role({1: 3, 5: 3, 2: -3, 6: -3, 0: 1, 4: 1, 3: -1, 7: -1})
NEAR_OF_MAIN = by_role({0: -1, 4: -1, 3: 1, 7: 1})
NEAR_TO_INNER = by_role({0: 2, 4: 2, 3: -2, 7: -2})
ON_OR_TO_OUTER = by_role({0: -2, 4: -2, 3: 2, 7: 2, 1: 2, 5: 2, 2: -2, 6: -2})
FAR_OR_ON_BY_ONE = by_role({1: -3, 5: -3, 2: 3, 6: 3, 0: -1, 4: -1, 3: 1, 7: 1})


def send(x, pairs):
    return lax.ppermute(x, AXES, pairs())


def together(*arrays):
    return lax.optimization_barrier(arrays)


def unit_of(raw_ref, rows):
    values = raw_ref[rows, :].astype(jnp.float32)
    scale = lax.rsqrt(jnp.sum(values * values, axis=-1, keepdims=True) + EPSILON)
    return values * scale, scale


def lower(raw_ref, low_ref):
    low_ref[...] = unit_of(raw_ref, slice(None))[0].astype(jnp.bfloat16)


def lower_one_of(chosen, this_ref, that_ref, low_ref):
    @pl.when(chosen)
    def _():
        lower(this_ref, low_ref)

    @pl.when(jnp.logical_not(chosen))
    def _():
        lower(that_ref, low_ref)


def terms(logits):
    shrunk = jnp.exp(-jnp.abs(logits))
    total = 1.0 + shrunk
    losses = jnp.maximum(logits, 0.0) + jnp.log(total)
    return losses, jnp.where(logits >= 0.0, 1.0, shrunk) / total


def folded(losses):
    out = losses[:, :LANES]
    for at in range(LANES, losses.shape[1], LANES):
        out = out + losses[:, at : at + LANES]
    return out


def product(left, right, left_dim, right_dim):
    return lax.dot_general(
        left, right, (((left_dim,), (right_dim,)), ((), ())), preferred_element_type=jnp.float32
    )


def partner_weights(numbers_ref, own_ref, partner_ref, loss_from, loss_to, counts):
    temper, bias = numbers_ref[0], numbers_ref[1]
    losses, chances = terms(temper * product(own_ref[...], partner_ref[...], 1, 1) + bias)
    loss_to[...] = loss_from[...] + counts * folded(losses)
    return (chances * temper).astype(jnp.bfloat16)


def pair(numbers_ref, own_ref, partner_ref, acc_from, acc_to, loss_from, loss_to, counts):
    weights = partner_weights(numbers_ref, own_ref, partner_ref, loss_from, loss_to, counts)
    acc_to[...] = acc_from[...] + product(weights, partner_ref[...], 1, 0)


def first_kernel(
    role_ref, numbers_ref, main, other, swapped,
    lows, units, scales, accs, loss_ref, weights_ref, low_ref,
):
    temper, bias = numbers_ref[0], numbers_ref[1]
    core = role_ref[0]
    count = main.shape[0]
    for side, raw in enumerate((main, other)):
        unit, scale = unit_of(raw, slice(None))
        units[side] = unit
        scales[side] = scale
        lows[side] = unit.astype(jnp.bfloat16)
    image_low, text_low = lows.at[core], lows.at[1 - core]
    logits = temper * product(image_low[...], text_low[...], 1, 1) + bias
    row = lax.broadcasted_iota(jnp.int32, (count, count), 0)
    column = lax.broadcasted_iota(jnp.int32, (count, count), 1)
    same = row == column
    losses, chances = terms(jnp.where(same, -logits, logits))
    loss_ref[...] = folded(losses)
    weights = (jnp.where(same, -chances, chances) * temper).astype(jnp.bfloat16)
    weights_ref[...] = weights
    accs[core] = product(weights, text_low[...], 1, 0)
    accs[1 - core] = product(weights_ref[...], image_low[...], 0, 0)
    lower(swapped, low_ref)
    pair(
        numbers_ref, lows.at[1], low_ref, accs.at[1], accs.at[1], loss_ref, loss_ref, core.astype(jnp.float32)
    )


def late_block_kernel(role_ref, lows, second, late_low):
    outer = role_ref[0] == role_ref[1]

    @pl.when(outer)
    def _():
        lower(second, late_low)

    @pl.when(jnp.logical_not(outer))
    def _():
        late_low[...] = lows[0]


def middle_kernel(
    role_ref, numbers_ref, lows, near_main, second, of_other, accs_in, loss_in, accs, loss_ref, low_ref
):
    on_main = 1.0 - role_ref[0].astype(jnp.float32)
    lower_one_of(role_ref[0] == role_ref[1], near_main, of_other, low_ref)
    pair(numbers_ref, lows.at[0], low_ref, accs_in.at[0], accs.at[0], loss_in, loss_ref, on_main)
    lower(second, low_ref)
    pair(numbers_ref, lows.at[0], low_ref, accs.at[0], accs.at[0], loss_ref, loss_ref, on_main)
    accs[1] = accs_in[1]


def close_side(
    side, core, numbers_ref, lows, units, scales, accs, partner_ref, loss_from, loss_to,
    image_out, text_out, weights_ref, done_ref, sems,
):
    counts = (side == core).astype(jnp.float32)
    weights_ref[...] = partner_weights(numbers_ref, lows.at[side], partner_ref, loss_from, loss_to, counts)

    def finish_into(out):
        copies = []
        for k in range(done_ref.shape[0] // STRIP):
            rows = pl.ds(k * STRIP, STRIP)
            grad = accs[side, rows, :] + product(weights_ref[rows, :], partner_ref[...], 1, 0)
            unit = units[side, rows, :]
            along = jnp.sum(unit * grad, axis=-1, keepdims=True)
            done_ref[rows, :] = scales[side, rows, :] * (grad - unit * along)
            copies.append(pltpu.make_async_copy(done_ref.at[rows, :], out.at[rows, :], sems.at[k]))
            copies[-1].start()
        for copy in copies:
            copy.wait()

    @pl.when(side == core)
    def _():
        finish_into(image_out)

    @pl.when(side != core)
    def _():
        finish_into(text_out)


def early_kernel(
    role_ref, numbers_ref, lows, units, scales, of_other, by_two, to_inner, accs_in, loss_in,
    image_out, text_out, accs, loss_ref, low_ref, weights_ref, done_ref, sems,
):
    outer = role_ref[0] == role_ref[1]
    lower_one_of(outer, by_two, to_inner, low_ref)
    accs[0] = accs_in[0]
    pair(
        numbers_ref, lows.at[1], low_ref, accs_in.at[1], accs.at[1], loss_in, loss_ref,
        role_ref[0].astype(jnp.float32),
    )
    lower_one_of(outer, of_other, by_two, low_ref)
    close_side(
        jnp.where(outer, 0, 1), role_ref[0], numbers_ref, lows, units, scales, accs, low_ref,
        loss_ref, loss_ref, image_out, text_out, weights_ref, done_ref, sems,
    )


def late_kernel(
    role_ref, numbers_ref, lows, units, scales, accs, late_low, loss_in, image_in, text_in,
    image_out, text_out, row_loss, loss_ref, weights_ref, done_ref, sems,
):
    outer = role_ref[0] == role_ref[1]
    close_side(
        jnp.where(outer, 1, 0), role_ref[0], numbers_ref, lows, units, scales, accs, late_low,
        loss_in, loss_ref, image_out, text_out, weights_ref, done_ref, sems,
    )
    row_loss[...] = jnp.sum(loss_ref[...].T, axis=0, keepdims=True)


def call(kernel, in_kinds, outs, scratch=(), aliases=None):
    kinds = {
        "s": pl.BlockSpec(memory_space=pltpu.SMEM),
        "v": pl.BlockSpec(memory_space=pltpu.VMEM),
        "a": pl.BlockSpec(memory_space=pl.ANY),
    }
    return pl.pallas_call(
        kernel,
        in_specs=[kinds[k] for k in in_kinds],
        out_specs=[kinds[k] for k, _, _ in outs],
        out_shape=[jax.ShapeDtypeStruct(shape, dtype) for _, shape, dtype in outs],
        scratch_shapes=list(scratch),
        input_output_aliases=aliases or {},
        compiler_params=pltpu.CompilerParams(vmem_limit_bytes=24 * 1024 * 1024),
    )


def body(image_emb, text_emb, log_temp, bias):
    rows, width = image_emb.shape
    place = lax.axis_index(AXES)
    core = (place // 2) % 2
    role = jnp.stack([core, place % 2]).astype(jnp.int32)
    numbers = jnp.stack([jnp.exp(log_temp), bias])
    is_core_1 = core == 1
    other, image_late, text_late = together(jnp.where(is_core_1, image_emb, text_emb), image_emb, text_emb)
    main = jnp.where(is_core_1, text_late, image_late)

    swapped = send(other, SWAP)
    of_other = send(other, OF_OTHER)
    second = send(main, SECOND)
    near_main = send(main, NEAR_OF_MAIN)

    f32, low = jnp.float32, jnp.bfloat16
    whole, partial, both = (rows, width), (rows, LANES), (2, rows, width)
    lows, units, scales, accs, loss = call(
        first_kernel,
        "ssvvv",
        [("v", both, low), ("v", both, f32), ("v", (2, rows, 1), f32), ("v", both, f32), ("v", partial, f32)],
        [pltpu.VMEM((rows, rows), low), pltpu.VMEM(whole, low)],
    )(role, numbers, main, other, swapped)

    second, near_main, loss = together(second, near_main, loss)
    (late_low,) = call(late_block_kernel, "svv", [("v", whole, low)])(role, lows, second)
    of_other, late_low = together(of_other, late_low)
    by_two = send(of_other, ON_OR_TO_OUTER)
    late_low = send(late_low, FAR_OR_ON_BY_ONE)
    to_inner = send(near_main, NEAR_TO_INNER)

    accs, loss = call(
        middle_kernel,
        "ssvvvvvv",
        [("v", both, f32), ("v", partial, f32)],
        [pltpu.VMEM(whole, low)],
        {6: 0, 7: 1},
    )(role, numbers, lows, near_main, second, of_other, accs, loss)

    copy_sems = pltpu.SemaphoreType.DMA((rows // STRIP,))
    grad_image, grad_text, accs, loss = call(
        early_kernel,
        "ssvvvvvvvv",
        [("a", whole, f32), ("a", whole, f32), ("v", both, f32), ("v", partial, f32)],
        [pltpu.VMEM(whole, low), pltpu.VMEM((rows, rows), low), pltpu.VMEM(whole, f32), copy_sems],
        {8: 2, 9: 3},
    )(role, numbers, lows, units, scales, of_other, by_two, to_inner, accs, loss)
    grad_image, grad_text, row_loss = call(
        late_kernel,
        "ssvvvvvvaa",
        [("a", whole, f32), ("a", whole, f32), ("v", (1, rows), f32)],
        [pltpu.VMEM(partial, f32), pltpu.VMEM((rows, rows), low), pltpu.VMEM(whole, f32), copy_sems],
        {8: 0, 9: 1},
    )(role, numbers, lows, units, scales, accs, late_low, loss, grad_image, grad_text)
    return (row_loss.reshape(rows), grad_image, grad_text)


def solution(mesh):
    return jax.shard_map(
        body,
        mesh=mesh,
        in_specs=(P(AXES, None), P(AXES, None), P(), P()),
        out_specs=(P(AXES), P(AXES, None), P(AXES, None)),
        check_vma=False,
    )
```
